128 devices in a mesh: row: 8 (over y, x_hi), col: 16 (over x_lo, z, core).
Axes of the slice: x: 4 (x_hi: 2, x_lo: 2; x = x_hi * 2 + x_lo), y: 4, z: 4, core: 2. Of those that a mesh axis runs over, the one named last changes fastest.
Arguments:
- queries: bfloat16 [128, 512, 1536], P('row', 'col'), may hold values from -101 to 101
- fresh_keys: bfloat16 [128, 512, 1536], P('row', 'col'), may hold values from -7.2 to 7.2
- fresh_values: bfloat16 [128, 512, 1536], P('row', 'col'), may hold values from -16 to 16
- stale_keys: bfloat16 [128, 512, 1536], P('row', 'col'), may hold values from -7.1875 to 7.1875
- stale_values: bfloat16 [128, 512, 1536], P('row', 'col'), may hold values from -16 to 16
- weight_out: bfloat16 [1536, 3072], replicated, may hold values from -0.15625 to 0.15625
- gate: float32 [3072], replicated, may hold values from 0.5 to 4
- far_tiles: int32 [128, 80], replicated, may hold values from -1 to 127, as said below
- far_blocks: int32 [128, 80], replicated, may hold values from 0 to 63
- far_count: int32 [128], replicated, may hold values from 40 to 80, as said below
Outputs:
- branch_out: bfloat16 [128, 512, 3072], P('row', 'col')
The draws below stay inside these ranges and needn't reach their ends.
Inputs may be any that keep to these rules, and one draw needn't show every extreme that they name: `far_tiles`: row t lists far_count[t] different tiles, none of them t and none of the tiles that touch t by a side or a corner; its other entries are -1. `far_blocks`: entries k >= far_count[t] of row t are not read. `far_count`: some tile reads exactly 80 far blocks.
All inputs are finite; a program needn't handle non-finite values.
Results may differ from the reference program's by a relative error of at most 0.0054.
Values may be sent and summed in bfloat16 or wider, within the bound.
A program may use at most 192 MiB of HBM per device.

```python
import math
import jax
import jax.numpy as jnp
from jax import lax

D = 3072
HEADS = 12
HD = 128
TH = 16
TW = 32
R = 6
BLK = 8
INNER = 1536
TILES = 128
TILE_COLS = 16
GRID_ROWS = 128
GRID_COLS = 512
NBLK = 64
FAR_MAX = 80
N_ROW = 8
N_COL = 16


def shared_keys(key):
    base = jax.random.normal(key, (GRID_ROWS, GRID_COLS, INNER), jnp.float32)
    return jnp.clip(base, -6.0, 6.0) * 1.2


def draw_queries(key, part):
    base = shared_keys(key)
    key = jax.random.fold_in(key, 2)
    own_draw = jnp.clip(jax.random.normal(key, base.shape, jnp.float32), -6.0, 6.0) * 1.2
    return own_draw.astype(jnp.bfloat16)


def draw_fresh_keys(key, part):
    base = shared_keys(key)
    return base.astype(jnp.bfloat16)


def far_lists(key):
    key_order, key_count, key_top = jax.random.split(key, 3)
    tile_ids = jnp.arange(TILES, dtype=jnp.int32)
    tile_row = tile_ids // TILE_COLS
    tile_col = tile_ids % TILE_COLS
    beside = (jnp.abs(tile_row[:, None] - tile_row[None, :]) <= 1) & (jnp.abs(tile_col[:, None] - tile_col[None, :]) <= 1)
    rank_keys = jax.random.randint(key_order, (TILES, TILES), 0, 4096, dtype=jnp.int32) * TILES + tile_ids[None, :]
    rank_keys = jnp.where(beside, rank_keys + 4096 * TILES, rank_keys)
    ranked = jnp.argsort(rank_keys, axis=1, stable=True)[:, :FAR_MAX].astype(jnp.int32)
    counts = jax.random.randint(key_count, (TILES,), FAR_MAX // 2, FAR_MAX + 1, dtype=jnp.int32)
    busiest = jax.random.randint(key_top, (), 0, TILES, dtype=jnp.int32)
    counts = jnp.where(tile_ids == busiest, FAR_MAX, counts).astype(jnp.int32)
    listed = jnp.where(jnp.arange(FAR_MAX, dtype=jnp.int32)[None, :] < counts[:, None], ranked, -1)
    return (listed.astype(jnp.int32), counts)


def draw_far_tiles(key, part):
    listed, counts = far_lists(key)
    return listed


def draw_far_count(key, part):
    listed, counts = far_lists(key)
    return counts


def plant(result, stream_key, low, top_value):
    shape = result.shape
    spot = [jax.random.randint(jax.random.fold_in(stream_key, axis), (), 0, shape[axis]) for axis in range(len(shape))]
    result = result.at[tuple(spot)].set(low)
    longest = shape.index(max(shape))
    spot[longest] = (spot[longest] + 1) % shape[longest]
    return result.at[tuple(spot)].set(top_value)


def block_levels(stream_key, dims, cuts, low, high):
    def one(axis_at, parts):
        steps = jax.random.uniform(jax.random.fold_in(jax.random.fold_in(stream_key, 6), axis_at), (parts,), jnp.float32, low / len(cuts), high / len(cuts))
        return jnp.repeat(jnp.exp(steps), dims[axis_at] // parts).reshape((-1,) + (1,) * (len(dims) - axis_at - 1))

    factor_of = one(*cuts[0])
    for cut in cuts[1:]:
        factor_of = factor_of * one(*cut)
    return factor_of


def normal_values(own_key, dims, deviation, limit, shards=(), kind=jnp.bfloat16):
    gain = block_levels(own_key, dims, shards, -0.22, 0.18) if shards else 1.0
    drawn = jax.random.normal(own_key, dims, jnp.float32) * deviation * gain
    return jnp.minimum(jnp.maximum(drawn, -limit), limit).astype(kind)


def setup_inputs(seed: int = 0) -> dict:
    key_list = jax.random.split(jax.random.key(seed), 11)
    return {
        "queries": draw_queries(jax.random.fold_in(key_list[10], 71), 0),
        "fresh_keys": draw_fresh_keys(jax.random.fold_in(key_list[10], 71), 0),
        "fresh_values": normal_values(key_list[2], (GRID_ROWS, GRID_COLS, INNER), 3.0, 16.0, ((0, 8), (1, 16))),
        "stale_keys": normal_values(key_list[3], (GRID_ROWS, GRID_COLS, INNER), 1.2, 7.1875, ((0, 8), (1, 16))),
        "stale_values": normal_values(key_list[4], (GRID_ROWS, GRID_COLS, INNER), 3.0, 16.0, ((0, 8), (1, 16))),
        "weight_out": normal_values(key_list[5], (INNER, D), INNER ** -0.5, 0.15625),
        "gate": jnp.clip(jnp.exp(jax.random.uniform(key_list[6], (D,), jnp.float32, math.log(0.5), math.log(4.0))), 0.5, 4.0),
        "far_tiles": draw_far_tiles(jax.random.fold_in(key_list[10], 71), 0),
        "far_blocks": plant(jax.random.randint(key_list[8], (TILES, FAR_MAX), 0, NBLK), jax.random.fold_in(key_list[8], 1), 0, NBLK - 1).astype(jnp.int32),
        "far_count": draw_far_count(jax.random.fold_in(key_list[10], 71), 0),
    }


def attend_rows(query_rows, key_rows, value_rows, allowed):
    query_heads = query_rows.astype(jnp.float32).reshape(query_rows.shape[0], HEADS, HD)
    key_heads = key_rows.astype(jnp.float32).reshape(key_rows.shape[0], HEADS, HD)
    value_heads = value_rows.astype(jnp.float32).reshape(value_rows.shape[0], HEADS, HD)
    scores = jnp.einsum("qhd,khd->hqk", query_heads, key_heads) * (HD ** -0.5)
    scores = jnp.where(allowed[None], scores, -jnp.inf)
    peak = jnp.max(scores, axis=2, keepdims=True)
    weights = jnp.exp(scores - peak)
    denominator = jnp.sum(weights, axis=2)
    rounded = lax.optimization_barrier(weights.astype(jnp.bfloat16)).astype(jnp.float32)
    blended = jnp.einsum("hqk,khd->qhd", rounded, value_heads)
    attended = (blended / denominator.T[:, :, None]).astype(jnp.bfloat16)
    return attended.reshape(query_rows.shape[0], HEADS * HD)


def window_mask(start_pos, query_count, key_span, radius, extent):
    query_pos = start_pos + jnp.arange(query_count, dtype=jnp.int32)
    key_pos = start_pos - radius + jnp.arange(key_span, dtype=jnp.int32)
    near_enough = jnp.abs(key_pos[None, :] - query_pos[:, None]) <= radius
    return near_enough & (key_pos[None, :] >= 0) & (key_pos[None, :] < extent)


def reference(queries, fresh_keys, fresh_values, stale_keys, stale_values, weight_out, gate, far_tiles, far_blocks, far_count):
    padding = ((R, R), (R, R), (0, 0))
    keys_padded = jnp.pad(fresh_keys, padding)
    values_padded = jnp.pad(fresh_values, padding)
    group_rows = 8 if TH % 8 == 0 else TH
    gate_row = gate

    def one_tile(tile_id):
        tile_row = (tile_id // TILE_COLS).astype(jnp.int32)
        tile_col = (tile_id % TILE_COLS).astype(jnp.int32)
        top_row = tile_row * TH
        left_col = tile_col * TW
        owners = far_tiles[tile_id]
        is_live = jnp.arange(FAR_MAX, dtype=jnp.int32) < far_count[tile_id]
        safe_owner = jnp.where(is_live, owners, 0)
        flat_pos = far_blocks[tile_id][:, None] * BLK + jnp.arange(BLK, dtype=jnp.int32)[None, :]
        far_rows = (safe_owner // TILE_COLS)[:, None] * TH + flat_pos // TW
        far_cols = (safe_owner % TILE_COLS)[:, None] * TW + flat_pos % TW
        far_k = stale_keys[far_rows, far_cols].reshape(FAR_MAX * BLK, INNER)
        far_v = stale_values[far_rows, far_cols].reshape(FAR_MAX * BLK, INNER)
        far_live = jnp.repeat(is_live, BLK)
        col_mask = window_mask(left_col, TW, TW + 2 * R, R, GRID_COLS)
        pieces = []
        for start_row in range(0, TH, group_rows):
            query_rows = lax.dynamic_slice(queries, (top_row + start_row, left_col, jnp.int32(0)), (group_rows, TW, INNER)).reshape(group_rows * TW, INNER)
            near_k = lax.dynamic_slice(keys_padded, (top_row + start_row, left_col, jnp.int32(0)), (group_rows + 2 * R, TW + 2 * R, INNER)).reshape(-1, INNER)
            near_v = lax.dynamic_slice(values_padded, (top_row + start_row, left_col, jnp.int32(0)), (group_rows + 2 * R, TW + 2 * R, INNER)).reshape(-1, INNER)
            row_mask = window_mask(top_row + start_row, group_rows, group_rows + 2 * R, R, GRID_ROWS)
            near_mask = (row_mask[:, None, :, None] & col_mask[None, :, None, :]).reshape(group_rows * TW, -1)
            allowed = jnp.concatenate([near_mask, jnp.broadcast_to(far_live[None, :], (group_rows * TW, FAR_MAX * BLK))], axis=1)
            key_rows = jnp.concatenate([near_k, far_k], axis=0)
            value_rows = jnp.concatenate([near_v, far_v], axis=0)
            pieces.append(attend_rows(query_rows, key_rows, value_rows, allowed))
        attended = jnp.concatenate(pieces, axis=0)
        projected = jnp.dot(attended, weight_out, preferred_element_type=jnp.float32)
        return (projected * gate_row[None, :]).astype(jnp.bfloat16)

    tiles_out = lax.map(one_tile, jnp.arange(TILES, dtype=jnp.int32))
    tiles_out = tiles_out.reshape(N_ROW, N_COL, TH, TW, D).transpose(0, 2, 1, 3, 4)
    return tiles_out.reshape(GRID_ROWS, GRID_COLS, D)
```

```python
import jax
import jax.numpy as jnp
from jax import lax
from jax.experimental import pallas as pl
from jax.experimental.pallas import tpu as pltpu
from jax.sharding import PartitionSpec as P

HD = 128
R = 6
BLK = 8
ROWS = 8
COLS = 16
TH = 16
TW = 32
HALF = 256
LOW = -1e30
SCALE = HD ** (-0.5) * 1.4426950408889634
MESH = pl.DeviceIdType.MESH

CLOSE = 29
EDGE = [(i, f, e) for i in (-1, 0, 1) for f in (0, 1) for e in (-1, 1)] + [(-1, 0, 0), (1, 0, 0)]
UNUSED = CLOSE + len(EDGE)
MAIN = UNUSED + 1
MIX = 25
SLOTS = 128
N_MAIN = SLOTS - MAIN
MID = COLS // 2
GROUPS = ((0, 48), (48, 32), (80, 32), (112, 16))
EARLY, LATE = 3, 4


def blend(late, before, after):
    return before + late * (after - before)


def close_offset(j):
    dr = blend(j // 24, 2 + 2 * (j % 3), 0)
    e = blend(j // 24, j // 3, j - 22)
    return dr, 0, e


def edge_offset(i):
    last = i // 12
    return blend(last, i // 4 - 1, 2 * (i - 12) - 1), blend(last, i // 2 % 2, 0), blend(last, 2 * (i % 2) - 1, 0)


def main_offset(p):
    i = MIX * p % N_MAIN
    straight = i // 58
    k = i - 40
    e1 = blend(i // 40, i // 5, k // 3 + (k // 3 + 5) // 6)
    dr1 = blend(i // 40, 2 + i % 5, 7 + k % 3)
    k = i - 58
    e2 = blend(i // 74, k // 2, 2 + (k - 16) // 2)
    dr2 = blend(i // 74, 3 + 2 * (k % 2), 7 + 2 * (k % 2))
    return blend(straight, dr1, dr2), 1 - straight, blend(straight, e1, e2)


def tile_at(row, col, dr, f, e):
    return (row + dr + 2 * ROWS) % ROWS, (col // MID + f + 2) % 2 * MID + (col % MID + e + 2 * MID) % MID


ROW_AT, COL_AT, PAD_AT, DEAD_AT = 0, TH + 2 * R, TH + TW + 4 * R, TH + TW + 4 * R + 1

NORTH, SOUTH, WEST, EAST, NW, NE, SW, SE = range(8)
BAND = R * TW
CORNER = 48
SIDE = TH * R
STRIP = SIDE + 2 * CORNER
OWN_SPAN = (TH - 2) * TW


def kernel(
    q_hbm, k_hbm, v_hbm, sk_hbm, sv_hbm, far_lists, block_of, att_hbm,
    q_ref, k_ref, v_ref, sk_ref, sv_ref,
    kn_ref, ks_ref, kw_ref, ke_ref, vn_ref, vs_ref, vw_ref, ve_ref,
    pack_ref, side_ref, corner_ref,
    far_ref, stage_ref, acc_ref, m_ref, l_ref, query_marks, own_marks, north_marks, south_marks, west_marks, east_marks, far_marks,
    live_ref, att_ref,
    load_sem, halo_send, halo_recv, far_send, far_recv, edge_send, edge_recv, out_sem,
):
    heads = q_ref.shape[1] // HD
    row = lax.axis_index("row")
    col = lax.axis_index("col")
    has_n, has_s = row > 0, row < ROWS - 1
    has_w, has_e = col > 0, col < COLS - 1
    exists = {
        NORTH: has_n, SOUTH: has_s, WEST: has_w, EAST: has_e,
        NW: has_n & has_w, NE: has_n & has_e, SW: has_s & has_w, SE: has_s & has_e,
    }

    crossing = {NW: col == MID - 1, SW: col == MID - 1, NE: col == MID, SE: col == MID}

    def halo_copies(piece, straight=False):
        up, down = (row - 1 + ROWS) % ROWS, (row + 1) % ROWS
        left, right = (col - 1 + COLS) % COLS, (col + 1) % COLS
        lower, upper = pl.ds(TH - R, R), pl.ds(0, R)
        top, middle, bottom = pl.ds(0, CORNER), pl.ds(CORNER, SIDE), pl.ds(CORNER + SIDE, CORNER)
        plan = {
            NORTH: (has_s, (down, col), (k_hbm.at[lower], v_hbm.at[lower]), (kn_ref, vn_ref)),
            SOUTH: (has_n, (up, col), (k_hbm.at[upper], v_hbm.at[upper]), (ks_ref, vs_ref)),
            WEST: (has_e, (row, right), (side_ref.at[0], side_ref.at[1]), (kw_ref.at[middle], vw_ref.at[middle])),
            EAST: (has_w, (row, left), (side_ref.at[2], side_ref.at[3]), (ke_ref.at[middle], ve_ref.at[middle])),
            NW: (has_n & has_e, (row, right), (corner_ref.at[0], corner_ref.at[1]), (kw_ref.at[top], vw_ref.at[top])),
            NE: (has_n & has_w, (row, left), (corner_ref.at[2], corner_ref.at[3]), (ke_ref.at[top], ve_ref.at[top])),
            SW: (has_s & has_e, (row, right), (corner_ref.at[4], corner_ref.at[5]),
                 (kw_ref.at[bottom], vw_ref.at[bottom])),
            SE: (has_s & has_w, (row, left), (corner_ref.at[6], corner_ref.at[7]),
                 (ke_ref.at[bottom], ve_ref.at[bottom])),
        }
        sends, target, srcs, dsts = plan[piece]
        if piece in crossing:
            if straight:
                sends = crossing[piece] & (has_s if piece in (NW, NE) else has_n)
                target = (down if piece in (NW, NE) else up, target[1])
            else:
                sends = sends & jnp.logical_not(crossing[piece])
        copies = [
            pltpu.make_async_remote_copy(
                src_ref=src, dst_ref=dst,
                send_sem=halo_send.at[2 * piece + i], recv_sem=halo_recv.at[2 * piece + i],
                device_id=target, device_id_type=MESH,
            )
            for i, (src, dst) in enumerate(zip(srcs, dsts))
        ]
        return sends, copies

    def start_halo(piece, straight=False):
        sends, copies = halo_copies(piece, straight)

        @pl.when(sends)
        def _():
            for copy in copies:
                copy.start()

    def wait_halo(piece):
        _, copies = halo_copies(piece)

        @pl.when(exists[piece])
        def _():
            for copy in copies:
                copy.wait_recv()

    def wait_halo_sent(piece, straight=False):
        sends, copies = halo_copies(piece, straight)

        @pl.when(sends)
        def _():
            for copy in copies:
                copy.wait_send()

    start_halo(NORTH)
    start_halo(SOUTH)

    loads = [
        pltpu.make_async_copy(src, dst, load_sem.at[i])
        for i, (src, dst) in enumerate(
            ((sk_hbm, sk_ref), (sv_hbm, sv_ref), (k_hbm, k_ref), (v_hbm, v_ref), (q_hbm, q_ref))
        )
    ]
    for load in loads:
        load.start()

    def far_copy(slot, target, send_sem, recv_sem):
        return pltpu.make_async_remote_copy(
            src_ref=stage_ref.at[slot], dst_ref=far_ref.at[slot], send_sem=send_sem, recv_sem=recv_sem,
            device_id=target, device_id_type=MESH,
        )

    def fill(slot, target):
        block = block_of[target[0] * COLS + target[1]]
        pair, odd = lax.shift_right_logical(block, 1), block & 1
        both = []
        for ref in (sk_ref, sv_ref):
            rows = ref[pair].astype(jnp.float32)
            both.append(jnp.where(odd == 1, rows[BLK:], rows[:BLK]))
        stage_ref[slot] = jnp.concatenate(both, axis=0).astype(jnp.bfloat16)

    def send_far(slot, offset, sem):
        target = tile_at(row, col, *offset)
        fill(slot, target)
        far_copy(slot, target, far_send, far_recv.at[sem]).start()

    loads[0].wait()
    loads[1].wait()

    @pl.loop(0, CLOSE)
    def _(j):
        send_far(j, close_offset(j), 0)

    def send_main(p):
        send_far(MAIN + p, main_offset(p), (MAIN + p - 16) // 32)

    def touches(dr, other):
        return (row + dr >= 0) & (row + dr < ROWS) & (other[1] - col >= -1) & (other[1] - col <= 1)

    def edge(i):
        dr, f, e = EDGE[i]
        target, origin = tile_at(row, col, dr, f, e), tile_at(row, col, -dr, -f, -e)
        copy = far_copy(CLOSE + i, target, edge_send.at[i], edge_recv.at[i])
        return target, jnp.logical_not(touches(dr, target)), jnp.logical_not(touches(-dr, origin)), copy

    for i in range(len(EDGE)):
        target, sends, receives, copy = edge(i)

        @pl.when(sends)
        def _(i=i, target=target, copy=copy):
            fill(CLOSE + i, target)
            copy.start()

        @pl.when(jnp.logical_not(receives))
        def _(i=i):
            far_ref[CLOSE + i] = jnp.zeros(far_ref.shape[1:], far_ref.dtype)

    far_ref[UNUSED] = jnp.zeros(far_ref.shape[1:], far_ref.dtype)

    def pack(source, first, count, right, target):
        for r in range(count):
            if right:
                edge = source[first + r, TW - 16:].astype(jnp.float32)[16 - R:]
            else:
                edge = source[first + r, :16].astype(jnp.float32)[:R]
            pack_ref[pl.ds(r * R, R)] = edge
        if target.shape[0] > count * R:
            pack_ref[count * R:target.shape[0]] = jnp.zeros((target.shape[0] - count * R, pack_ref.shape[1]), jnp.float32)
        target[...] = pack_ref[:target.shape[0]].astype(jnp.bfloat16)

    loads[2].wait()
    loads[3].wait()
    for i, (ref, right) in enumerate(((k_ref, True), (v_ref, True), (k_ref, False), (v_ref, False))):
        pack(ref, 0, TH, right, side_ref.at[i])
    start_halo(WEST)
    start_halo(EAST)
    for i, piece in enumerate((NW, NE, SW, SE)):
        @pl.when(crossing[piece])
        def _(i=i, piece=piece):
            for n, ref in enumerate((k_ref, v_ref)):
                pack(ref, TH - R if piece in (NW, NE) else 0, R, piece in (NW, SW), corner_ref.at[2 * i + n])
        start_halo(piece, True)

    def clear(missing, refs):
        @pl.when(missing)
        def _():
            for ref in refs:
                ref[...] = jnp.zeros(ref.shape, ref.dtype)

    top, middle, bottom = pl.ds(0, CORNER), pl.ds(CORNER, SIDE), pl.ds(CORNER + SIDE, CORNER)
    clear(jnp.logical_not(has_n), [kn_ref, vn_ref])
    clear(jnp.logical_not(has_s), [ks_ref, vs_ref])
    clear(jnp.logical_not(has_w), [kw_ref.at[middle], vw_ref.at[middle]])
    clear(jnp.logical_not(has_e), [ke_ref.at[middle], ve_ref.at[middle]])
    clear(jnp.logical_not(exists[NW]), [kw_ref.at[top], vw_ref.at[top]])
    clear(jnp.logical_not(exists[SW]), [kw_ref.at[bottom], vw_ref.at[bottom]])
    clear(jnp.logical_not(exists[NE]), [ke_ref.at[top], ve_ref.at[top]])
    clear(jnp.logical_not(exists[SE]), [ke_ref.at[bottom], ve_ref.at[bottom]])

    def key_marks(keys, place):
        shape = (keys, HD)
        u, v, real = place(lax.broadcasted_iota(jnp.int32, shape, 0))
        lane = lax.broadcasted_iota(jnp.int32, shape, 1)
        on = (lane == u + R + ROW_AT) | (lane == v + R + COL_AT) | ((lane == PAD_AT) & jnp.logical_not(real))
        return jnp.where(on, 1.0, 0.0).astype(jnp.bfloat16)

    def make_query_marks():
        shape = (TH * TW, HD)
        query, lane = lax.broadcasted_iota(jnp.int32, shape, 0), lax.broadcasted_iota(jnp.int32, shape, 1)
        u, v = lane - ROW_AT - R, lane - COL_AT - R
        row_off = (jnp.abs(u - query // TW) > R) | (u + row * TH < 0) | (u + row * TH >= ROWS * TH)
        col_off = (jnp.abs(v - query % TW) > R) | (v + col * TW < 0) | (v + col * TW >= COLS * TW)
        low = ((lane < COL_AT) & row_off) | ((lane >= COL_AT) & (lane < PAD_AT) & col_off) | (lane == PAD_AT)
        return jnp.where(low, LOW, jnp.where(lane == DEAD_AT, 1.0, 0.0)).astype(jnp.bfloat16)

    def strip_place(first_col):
        def place(key):
            upper, lower = key < CORNER, key >= CORNER + SIDE
            start = jnp.where(upper, 0, jnp.where(lower, CORNER + SIDE, CORNER))
            first_row = jnp.where(upper, -R, jnp.where(lower, TH, 0))
            cell = key - start
            real = (cell < R * R) | jnp.logical_not(upper | lower)
            return first_row + cell // R, first_col + cell % R, real

        return place

    def band_place(first_row):
        return lambda key: (first_row + key // TW, key % TW, key >= 0)

    query_marks[...] = make_query_marks()
    own_marks[...] = key_marks(TH * TW, band_place(0))

    def lanes(h):
        return pl.ds(pl.multiple_of(h * HD, HD), HD)

    def across(half):
        return pl.ds(half * HALF, HALF)

    def scores(keys, query):
        return lax.dot_general(keys, query, (((1,), (1,)), ((), ())), preferred_element_type=jnp.float32)

    def mix(values, weights):
        return lax.dot_general(values, weights, (((0,), (0,)), ((), ())), preferred_element_type=jnp.float32)

    def absorb(h0, parts_of, first=False):
        chains = [(h0 + i, half) for i in (0, 1) for half in (0, 1)]

        def start(chain):
            h, half = chain
            query = jnp.concatenate([q_ref[across(half), lanes(h)], query_marks[across(half)]], axis=1)
            parts = parts_of(h, half)
            return [(scores(jnp.concatenate([keys, marks], axis=1), query), values) for keys, marks, values in parts]

        def finish(chain, parts):
            h, half = chain
            peak = jnp.max(parts[0][0], axis=0, keepdims=True)
            for raw, _ in parts[1:]:
                peak = jnp.maximum(peak, jnp.max(raw, axis=0, keepdims=True))
            if not first:
                before = m_ref[h, :, across(half)]
                peak = jnp.maximum(before, peak)
            total, mixed = None, None
            for raw, values in parts:
                weights = jnp.exp2((raw - peak) * SCALE)
                part = jnp.sum(weights, axis=0, keepdims=True)
                product = mix(values, weights.astype(jnp.bfloat16))
                total = part if total is None else total + part
                mixed = product if mixed is None else mixed + product
            if not first:
                fade = jnp.exp2((before - peak) * SCALE)
                total = l_ref[h, :, across(half)] * fade + total
                mixed = acc_ref[h, :, across(half)] * fade + mixed
            return peak, total, mixed

        results = []
        ready = start(chains[0])
        for n, chain in enumerate(chains):
            parts = ready
            if n + 1 < len(chains):
                ready = start(chains[n + 1])
            results.append(finish(chain, parts))
        for (h, half), found in zip(chains, results):
            m_ref[h, :, across(half)], l_ref[h, :, across(half)], acc_ref[h, :, across(half)] = found

    loads[4].wait()

    @pl.loop(0, heads, step=2)
    def _(h0):
        @pl.loop(0, 2 * EARLY)
        def _(j):
            send_main(h0 * EARLY + j)

        def parts_of(h, half):
            rows = pl.ds(half * 2, TH - 2)
            keys = k_ref[rows, :, lanes(h)].reshape(OWN_SPAN, HD)
            return [(keys, own_marks[pl.ds(half * 2 * TW, OWN_SPAN)], v_ref[rows, :, lanes(h)].reshape(OWN_SPAN, HD))]

        absorb(h0, parts_of, first=True)

    west_marks[...] = key_marks(STRIP, strip_place(-R))
    east_marks[...] = key_marks(STRIP, strip_place(TW))
    north_marks[...] = key_marks(BAND, band_place(-R))
    south_marks[...] = key_marks(BAND, band_place(TH))

    def far_sources():
        slot = lax.broadcasted_iota(jnp.int32, (far_lists.shape[0], SLOTS), 1)
        found = [
            jnp.where(slot < CLOSE, first, jnp.where(slot < MAIN, second, third))
            for first, second, third in zip(close_offset(slot), edge_offset(slot - CLOSE), main_offset(slot - MAIN))
        ]
        source = tile_at(row, col, *(-part for part in found))
        return jnp.where(slot == UNUSED, -2, source[0] * COLS + source[1]).astype(jnp.float32)

    tile = lax.broadcasted_iota(jnp.int32, far_lists.shape, 1)
    own_list = jnp.max(jnp.where(tile == row * COLS + col, far_lists[...].astype(jnp.float32), -1.0), axis=1, keepdims=True)
    listed = jnp.max(jnp.where(far_sources() == own_list, 0.0, LOW).astype(jnp.float32), axis=0, keepdims=True)
    live_ref[...] = jnp.broadcast_to(listed, live_ref.shape).T

    @pl.loop(0, SLOTS // 2)
    def _(pair):
        both = [jnp.broadcast_to(live_ref[pl.ds(2 * pair + i, 1), :], (BLK, HD)) for i in (0, 1)]
        lane = lax.broadcasted_iota(jnp.int32, (2 * BLK, HD), 1)
        marks = jnp.where(lane == DEAD_AT, jnp.concatenate(both, axis=0), 0.0)
        far_marks[pl.ds(pl.multiple_of(pair * 2 * BLK, 2 * BLK), 2 * BLK)] = marks.astype(jnp.bfloat16)

    def use_far(group):
        first, count = GROUPS[group]
        regular = CLOSE + GROUPS[1][0] - MAIN if group == 0 else count
        part = far_ref.at[pl.ds(first, regular)]
        pltpu.make_async_remote_copy(
            src_ref=part, dst_ref=part, send_sem=far_send, recv_sem=far_recv.at[group],
            device_id=(row, (col + 1) % COLS), device_id_type=MESH,
        ).wait_recv()
        if group == 0:
            for i in range(len(EDGE)):
                _, _, receives, copy = edge(i)

                @pl.when(receives)
                def _(copy=copy):
                    copy.wait_recv()

        @pl.loop(0, heads, step=2)
        def _(h0):
            def parts_of(h, half):
                both = far_ref[pl.ds(first, count), :, lanes(h)].astype(jnp.float32)
                keys = both[:, :BLK].reshape(count * BLK, HD).astype(jnp.bfloat16)
                values = both[:, BLK:].reshape(count * BLK, HD).astype(jnp.bfloat16)
                return [(keys, far_marks[pl.ds(first * BLK, count * BLK)], values)]

            absorb(h0, parts_of)

    use_far(0)
    wait_halo(NORTH)
    wait_halo(SOUTH)
    for i, piece in enumerate((NW, NE, SW, SE)):
        @pl.when(jnp.logical_not(crossing[piece]))
        def _(i=i, piece=piece):
            for n, ref in enumerate((kn_ref, vn_ref) if piece in (NW, NE) else (ks_ref, vs_ref)):
                pack(ref, 0, R, piece in (NW, SW), corner_ref.at[2 * i + n])
        start_halo(piece)

    wait_halo(WEST)
    wait_halo(EAST)

    @pl.loop(0, heads, step=2)
    def _(h0):
        @pl.loop(0, 2 * LATE)
        def _(j):
            send_main(heads * EARLY + h0 * LATE + j)

        def parts_of(h, half):
            band_k, band_v, marks = ((kn_ref, vn_ref, north_marks), (ks_ref, vs_ref, south_marks))[half]
            found = [(band_k[:, :, lanes(h)].reshape(BAND, HD), marks[...], band_v[:, :, lanes(h)].reshape(BAND, HD))]
            for strip_k, strip_v, marks in ((kw_ref, vw_ref, west_marks), (ke_ref, ve_ref, east_marks)):
                found.append((strip_k[middle, lanes(h)], marks[middle], strip_v[middle, lanes(h)]))
            return found

        absorb(h0, parts_of)

    use_far(1)
    use_far(2)
    for piece in (NW, NE, SW, SE):
        wait_halo(piece)

    @pl.loop(0, heads, step=2)
    def _(h0):
        def parts_of(h, half):
            end = (top, bottom)[half]
            return [
                (strip_k[end, lanes(h)], marks[end], strip_v[end, lanes(h)])
                for strip_k, strip_v, marks in ((kw_ref, vw_ref, west_marks), (ke_ref, ve_ref, east_marks))
            ]

        absorb(h0, parts_of)

    use_far(3)

    @pl.loop(0, heads)
    def _(h):
        att_ref[:, lanes(h)] = (acc_ref[h] / l_ref[h]).T.astype(jnp.bfloat16)

    out_copy = pltpu.make_async_copy(att_ref, att_hbm, out_sem)
    out_copy.start()

    for piece in range(8):
        wait_halo_sent(piece)
        if piece in crossing:
            wait_halo_sent(piece, True)
    sent = stage_ref.at[pl.ds(0, CLOSE + N_MAIN)]
    pltpu.make_async_remote_copy(
        src_ref=sent, dst_ref=sent, send_sem=far_send, recv_sem=far_recv.at[0],
        device_id=(row, (col + 1) % COLS), device_id_type=MESH,
    ).wait_send()
    for i in range(len(EDGE)):
        _, sends, _, copy = edge(i)

        @pl.when(sends)
        def _(copy=copy):
            copy.wait_send()
    out_copy.wait()


def shards(
    queries, fresh_keys, fresh_values, stale_keys, stale_values, weight_out, gate, far_tiles, far_blocks, far_count
):
    inner = queries.shape[2]
    heads = inner // HD
    model = weight_out.shape[1]
    own = lax.axis_index("row") * COLS + lax.axis_index("col")
    block_of = jnp.sum(jnp.where(far_tiles == own, far_blocks, 0), axis=1)

    bf16, f32 = jnp.bfloat16, jnp.float32
    tokens = TH * TW
    any_spec = pl.BlockSpec(memory_space=pl.ANY)
    vmem_spec = pl.BlockSpec(memory_space=pltpu.VMEM)
    smem_spec = pl.BlockSpec(memory_space=pltpu.SMEM)
    band, strip = (R, TW, inner), (STRIP, inner)
    attended = pl.pallas_call(
        kernel,
        out_shape=jax.ShapeDtypeStruct((tokens, inner), bf16),
        in_specs=[any_spec] * 5 + [vmem_spec, smem_spec],
        out_specs=any_spec,
        scratch_shapes=[
            pltpu.VMEM((tokens, inner), bf16),
            pltpu.VMEM((TH, TW, inner), bf16),
            pltpu.VMEM((TH, TW, inner), bf16),
            pltpu.VMEM((tokens // 16, 16, inner), bf16),
            pltpu.VMEM((tokens // 16, 16, inner), bf16),
            pltpu.VMEM(band, bf16), pltpu.VMEM(band, bf16), pltpu.VMEM(strip, bf16), pltpu.VMEM(strip, bf16),
            pltpu.VMEM(band, bf16), pltpu.VMEM(band, bf16), pltpu.VMEM(strip, bf16), pltpu.VMEM(strip, bf16),
            pltpu.VMEM((SIDE, inner), f32),
            pltpu.VMEM((4, SIDE, inner), bf16),
            pltpu.VMEM((8, CORNER, inner), bf16),
            pltpu.VMEM((SLOTS, 2 * BLK, inner), bf16),
            pltpu.VMEM((SLOTS, 2 * BLK, inner), bf16),
            pltpu.VMEM((heads, HD, tokens), f32),
            pltpu.VMEM((heads, 1, tokens), f32),
            pltpu.VMEM((heads, 1, tokens), f32),
            pltpu.VMEM((tokens, HD), bf16),
            pltpu.VMEM((tokens, HD), bf16),
            pltpu.VMEM((BAND, HD), bf16),
            pltpu.VMEM((BAND, HD), bf16),
            pltpu.VMEM((STRIP, HD), bf16),
            pltpu.VMEM((STRIP, HD), bf16),
            pltpu.VMEM((SLOTS * BLK, HD), bf16),
            pltpu.VMEM((SLOTS, 128), f32),
            pltpu.VMEM((tokens, inner), bf16),
            pltpu.SemaphoreType.DMA((5,)),
            pltpu.SemaphoreType.DMA((16,)),
            pltpu.SemaphoreType.DMA((16,)),
            pltpu.SemaphoreType.DMA,
            pltpu.SemaphoreType.DMA((len(GROUPS),)),
            pltpu.SemaphoreType.DMA((len(EDGE),)),
            pltpu.SemaphoreType.DMA((len(EDGE),)),
            pltpu.SemaphoreType.DMA,
        ],
        compiler_params=pltpu.CompilerParams(has_side_effects=True, vmem_limit_bytes=57 * 1024 * 1024),
        name="attention",
    )(
        queries.reshape(tokens, inner), fresh_keys, fresh_values,
        stale_keys.reshape(-1, 16, inner), stale_values.reshape(-1, 16, inner), far_tiles.T, block_of,
    )
    projected = jnp.dot(attended, weight_out, preferred_element_type=jnp.float32)
    return (projected * gate[None, :]).astype(bf16).reshape(TH, TW, model)


def solution(mesh):
    tile = P("row", "col", None)
    return jax.shard_map(
        shards, mesh=mesh, in_specs=(tile,) * 5 + (P(),) * 5, out_specs=tile, check_vma=False,
    )
```

```python
import jax
import jax.numpy as jnp
from jax import lax
from jax.experimental import pallas as pl
from jax.experimental.pallas import tpu as pltpu
from jax.sharding import PartitionSpec as P

HD = 128
R = 6
BLK = 8
ROWS = 8
COLS = 16
TH = 16
TW = 32
HALF = 256
LOW = -1e30
SCALE = HD ** (-0.5) * 1.4426950408889634
MESH = pl.DeviceIdType.MESH

CLOSE = 29
EDGE = [(i, f, e) for i in (-1, 0, 1) for f in (0, 1) for e in (-1, 1)] + [(-1, 0, 0), (1, 0, 0)]
UNUSED = CLOSE + len(EDGE)
MAIN = UNUSED + 1
MIX = 25
SLOTS = 128
N_MAIN = SLOTS - MAIN
MID = COLS // 2
GROUPS = ((0, 48), (48, 32), (80, 32), (112, 16))
EARLY, LATE = 4, 36


def blend(late, before, after):
    return before + late * (after - before)


def close_offset(j):
    dr = blend(j // 24, 2 + 2 * (j % 3), 0)
    e = blend(j // 24, j // 3, j - 22)
    return dr, 0, e


def edge_offset(i):
    last = i // 12
    return blend(last, i // 4 - 1, 2 * (i - 12) - 1), blend(last, i // 2 % 2, 0), blend(last, 2 * (i % 2) - 1, 0)


def main_offset(p):
    i = MIX * p % N_MAIN
    straight = i // 58
    k = i - 40
    e1 = blend(i // 40, i // 5, k // 3 + (k // 3 + 5) // 6)
    dr1 = blend(i // 40, 2 + i % 5, 7 + k % 3)
    k = i - 58
    e2 = blend(i // 74, k // 2, 2 + (k - 16) // 2)
    dr2 = blend(i // 74, 3 + 2 * (k % 2), 7 + 2 * (k % 2))
    return blend(straight, dr1, dr2), 1 - straight, blend(straight, e1, e2)


def tile_at(row, col, dr, f, e):
    return (row + dr + 2 * ROWS) % ROWS, (col // MID + f + 2) % 2 * MID + (col % MID + e + 2 * MID) % MID


ROW_AT, COL_AT, PAD_AT, DEAD_AT = 0, TH + 2 * R, TH + TW + 4 * R, TH + TW + 4 * R + 1

NORTH, SOUTH, WEST, EAST, NW, NE, SW, SE = range(8)
BAND = R * TW
CORNER = 48
SIDE = TH * R
STRIP = SIDE + 2 * CORNER
OWN_SPAN = (TH - 2) * TW


def kernel(
    q_hbm, k_hbm, v_hbm, sk_hbm, sv_hbm, far_lists, block_of, att_hbm,
    q_ref, k_ref, v_ref, sk_ref, sv_ref,
    kn_ref, ks_ref, kw_ref, ke_ref, vn_ref, vs_ref, vw_ref, ve_ref,
    pack_ref, side_ref, corner_ref,
    far_ref, stage_ref, acc_ref, m_ref, l_ref, qt_ref, far_k, far_v, own_marks, north_marks, south_marks, west_marks, east_marks, far_marks,
    live_ref, att_ref,
    load_sem, halo_send, halo_recv, far_send, far_recv, edge_send, edge_recv, out_sem,
):
    heads = q_ref.shape[1] // HD
    row = lax.axis_index("row")
    col = lax.axis_index("col")
    has_n, has_s = row > 0, row < ROWS - 1
    has_w, has_e = col > 0, col < COLS - 1
    exists = {
        NORTH: has_n, SOUTH: has_s, WEST: has_w, EAST: has_e,
        NW: has_n & has_w, NE: has_n & has_e, SW: has_s & has_w, SE: has_s & has_e,
    }

    crossing = {NW: col == MID - 1, SW: col == MID - 1, NE: col == MID, SE: col == MID}

    def halo_copies(piece, straight=False):
        up, down = (row - 1 + ROWS) % ROWS, (row + 1) % ROWS
        left, right = (col - 1 + COLS) % COLS, (col + 1) % COLS
        lower, upper = pl.ds(TH - R, R), pl.ds(0, R)
        top, middle, bottom = pl.ds(0, CORNER), pl.ds(CORNER, SIDE), pl.ds(CORNER + SIDE, CORNER)
        plan = {
            NORTH: (has_s, (down, col), (k_hbm.at[lower], v_hbm.at[lower]), (kn_ref, vn_ref)),
            SOUTH: (has_n, (up, col), (k_hbm.at[upper], v_hbm.at[upper]), (ks_ref, vs_ref)),
            WEST: (has_e, (row, right), (side_ref.at[0], side_ref.at[1]), (kw_ref.at[middle], vw_ref.at[middle])),
            EAST: (has_w, (row, left), (side_ref.at[2], side_ref.at[3]), (ke_ref.at[middle], ve_ref.at[middle])),
            NW: (has_n & has_e, (row, right), (corner_ref.at[0], corner_ref.at[1]), (kw_ref.at[top], vw_ref.at[top])),
            NE: (has_n & has_w, (row, left), (corner_ref.at[2], corner_ref.at[3]), (ke_ref.at[top], ve_ref.at[top])),
            SW: (has_s & has_e, (row, right), (corner_ref.at[4], corner_ref.at[5]),
                 (kw_ref.at[bottom], vw_ref.at[bottom])),
            SE: (has_s & has_w, (row, left), (corner_ref.at[6], corner_ref.at[7]),
                 (ke_ref.at[bottom], ve_ref.at[bottom])),
        }
        sends, target, srcs, dsts = plan[piece]
        if piece in crossing:
            if straight:
                sends = crossing[piece] & (has_s if piece in (NW, NE) else has_n)
                target = (down if piece in (NW, NE) else up, target[1])
            else:
                sends = sends & jnp.logical_not(crossing[piece])
        copies = [
            pltpu.make_async_remote_copy(
                src_ref=src, dst_ref=dst,
                send_sem=halo_send.at[2 * piece + i], recv_sem=halo_recv.at[2 * piece + i],
                device_id=target, device_id_type=MESH,
            )
            for i, (src, dst) in enumerate(zip(srcs, dsts))
        ]
        return sends, copies

    def start_halo(piece, straight=False):
        sends, copies = halo_copies(piece, straight)

        @pl.when(sends)
        def _():
            for copy in copies:
                copy.start()

    def wait_halo(piece):
        _, copies = halo_copies(piece)

        @pl.when(exists[piece])
        def _():
            for copy in copies:
                copy.wait_recv()

    def wait_halo_sent(piece, straight=False):
        sends, copies = halo_copies(piece, straight)

        @pl.when(sends)
        def _():
            for copy in copies:
                copy.wait_send()

    start_halo(NORTH)
    start_halo(SOUTH)

    loads = [
        pltpu.make_async_copy(src, dst, load_sem.at[i])
        for i, (src, dst) in enumerate(
            ((sk_hbm, sk_ref), (sv_hbm, sv_ref), (k_hbm, k_ref), (v_hbm, v_ref), (q_hbm, q_ref))
        )
    ]
    for load in loads:
        load.start()

    def far_copy(slot, target, send_sem, recv_sem):
        return pltpu.make_async_remote_copy(
            src_ref=stage_ref.at[slot], dst_ref=far_ref.at[slot], send_sem=send_sem, recv_sem=recv_sem,
            device_id=target, device_id_type=MESH,
        )

    def fill(slot, target):
        block = block_of[target[0] * COLS + target[1]]
        pair, odd = lax.shift_right_logical(block, 1), block & 1
        both = []
        for ref in (sk_ref, sv_ref):
            rows = ref[pair].astype(jnp.float32)
            both.append(jnp.where(odd == 1, rows[BLK:], rows[:BLK]))
        stage_ref[slot] = jnp.concatenate(both, axis=0).astype(jnp.bfloat16)

    def send_far(slot, offset, sem):
        target = tile_at(row, col, *offset)
        fill(slot, target)
        far_copy(slot, target, far_send, far_recv.at[sem]).start()

    loads[0].wait()
    loads[1].wait()

    @pl.loop(0, CLOSE)
    def _(j):
        send_far(j, close_offset(j), 0)

    def send_main(p):
        send_far(MAIN + p, main_offset(p), (MAIN + p - 16) // 32)

    def touches(dr, other):
        return (row + dr >= 0) & (row + dr < ROWS) & (other[1] - col >= -1) & (other[1] - col <= 1)

    def edge(i):
        dr, f, e = EDGE[i]
        target, origin = tile_at(row, col, dr, f, e), tile_at(row, col, -dr, -f, -e)
        copy = far_copy(CLOSE + i, target, edge_send.at[i], edge_recv.at[i])
        return target, jnp.logical_not(touches(dr, target)), jnp.logical_not(touches(-dr, origin)), copy

    for i in range(len(EDGE)):
        target, sends, receives, copy = edge(i)

        @pl.when(sends)
        def _(i=i, target=target, copy=copy):
            fill(CLOSE + i, target)
            copy.start()

        @pl.when(jnp.logical_not(receives))
        def _(i=i):
            far_ref[CLOSE + i] = jnp.zeros(far_ref.shape[1:], far_ref.dtype)

    far_ref[UNUSED] = jnp.zeros(far_ref.shape[1:], far_ref.dtype)

    def pack(source, first, count, right, target):
        for r in range(count):
            if right:
                edge = source[first + r, TW - 16:].astype(jnp.float32)[16 - R:]
            else:
                edge = source[first + r, :16].astype(jnp.float32)[:R]
            pack_ref[pl.ds(r * R, R)] = edge
        if target.shape[0] > count * R:
            pack_ref[count * R:target.shape[0]] = jnp.zeros((target.shape[0] - count * R, pack_ref.shape[1]), jnp.float32)
        target[...] = pack_ref[:target.shape[0]].astype(jnp.bfloat16)

    loads[2].wait()
    loads[3].wait()
    for i, (ref, right) in enumerate(((k_ref, True), (v_ref, True), (k_ref, False), (v_ref, False))):
        pack(ref, 0, TH, right, side_ref.at[i])
    start_halo(WEST)
    start_halo(EAST)
    for i, piece in enumerate((NW, NE, SW, SE)):
        @pl.when(crossing[piece])
        def _(i=i, piece=piece):
            for n, ref in enumerate((k_ref, v_ref)):
                pack(ref, TH - R if piece in (NW, NE) else 0, R, piece in (NW, SW), corner_ref.at[2 * i + n])
        start_halo(piece, True)

    def clear(missing, refs):
        @pl.when(missing)
        def _():
            for ref in refs:
                ref[...] = jnp.zeros(ref.shape, ref.dtype)

    top, middle, bottom = pl.ds(0, CORNER), pl.ds(CORNER, SIDE), pl.ds(CORNER + SIDE, CORNER)
    clear(jnp.logical_not(has_n), [kn_ref, vn_ref])
    clear(jnp.logical_not(has_s), [ks_ref, vs_ref])
    clear(jnp.logical_not(has_w), [kw_ref.at[middle], vw_ref.at[middle]])
    clear(jnp.logical_not(has_e), [ke_ref.at[middle], ve_ref.at[middle]])
    clear(jnp.logical_not(exists[NW]), [kw_ref.at[top], vw_ref.at[top]])
    clear(jnp.logical_not(exists[SW]), [kw_ref.at[bottom], vw_ref.at[bottom]])
    clear(jnp.logical_not(exists[NE]), [ke_ref.at[top], ve_ref.at[top]])
    clear(jnp.logical_not(exists[SE]), [ke_ref.at[bottom], ve_ref.at[bottom]])

    def key_marks(keys, place):
        shape = (keys, HD)
        u, v, real = place(lax.broadcasted_iota(jnp.int32, shape, 0))
        lane = lax.broadcasted_iota(jnp.int32, shape, 1)
        on = (lane == u + R + ROW_AT) | (lane == v + R + COL_AT) | ((lane == PAD_AT) & jnp.logical_not(real))
        return jnp.where(on, 1.0, 0.0).astype(jnp.bfloat16)

    def make_query_marks():
        shape = (HD, TH * TW)
        lane, query = lax.broadcasted_iota(jnp.int32, shape, 0), lax.broadcasted_iota(jnp.int32, shape, 1)
        u, v = lane - ROW_AT - R, lane - COL_AT - R
        row_off = (jnp.abs(u - query // TW) > R) | (u + row * TH < 0) | (u + row * TH >= ROWS * TH)
        col_off = (jnp.abs(v - query % TW) > R) | (v + col * TW < 0) | (v + col * TW >= COLS * TW)
        low = ((lane < COL_AT) & row_off) | ((lane >= COL_AT) & (lane < PAD_AT) & col_off) | (lane == PAD_AT)
        return jnp.where(low, LOW, jnp.where(lane == DEAD_AT, 1.0, 0.0)).astype(jnp.bfloat16)

    def strip_place(first_col):
        def place(key):
            upper, lower = key < CORNER, key >= CORNER + SIDE
            start = jnp.where(upper, 0, jnp.where(lower, CORNER + SIDE, CORNER))
            first_row = jnp.where(upper, -R, jnp.where(lower, TH, 0))
            cell = key - start
            real = (cell < R * R) | jnp.logical_not(upper | lower)
            return first_row + cell // R, first_col + cell % R, real

        return place

    def band_place(first_row):
        return lambda key: (first_row + key // TW, key % TW, key >= 0)

    own_marks[...] = key_marks(TH * TW, band_place(0))

    def lanes(h):
        return pl.ds(pl.multiple_of(h * HD, HD), HD)

    def across(half):
        return pl.ds(0, 2 * HALF) if half is None else pl.ds(half * HALF, HALF)

    def scores(keys, query):
        return jnp.dot(keys, query, preferred_element_type=jnp.float32)

    def mix(values, weights):
        return lax.dot_general(values, weights, (((0,), (0,)), ((), ())), preferred_element_type=jnp.float32)

    def absorb(h0, parts_of, first=False, halves=(0, 1)):
        chains = [(h0 + i, half) for i in (0, 1) for half in halves]

        def start(chain):
            h, half = chain
            query = qt_ref[h, :, across(half)]
            parts = parts_of(h, half)
            return [(scores(jnp.concatenate([keys, marks], axis=1), query), values) for keys, marks, values in parts]

        def finish(chain, parts):
            h, half = chain
            peak = jnp.max(parts[0][0], axis=0, keepdims=True)
            for raw, _ in parts[1:]:
                peak = jnp.maximum(peak, jnp.max(raw, axis=0, keepdims=True))
            if not first:
                before = m_ref[h, :, across(half)]
                peak = jnp.maximum(before, peak)
            total, mixed = None, None
            for raw, values in parts:
                weights = jnp.exp2((raw - peak) * SCALE)
                part = jnp.sum(weights, axis=0, keepdims=True)
                product = mix(values, weights.astype(jnp.bfloat16))
                total = part if total is None else total + part
                mixed = product if mixed is None else mixed + product
            if not first:
                fade = jnp.exp2((before - peak) * SCALE)
                total = l_ref[h, :, across(half)] * fade + total
                mixed = acc_ref[h, :, across(half)] * fade + mixed
            return peak, total, mixed

        results = []
        ready = start(chains[0])
        for n, chain in enumerate(chains):
            parts = ready
            if n + 1 < len(chains):
                ready = start(chains[n + 1])
            results.append(finish(chain, parts))
        for (h, half), found in zip(chains, results):
            m_ref[h, :, across(half)], l_ref[h, :, across(half)], acc_ref[h, :, across(half)] = found

    loads[4].wait()
    marks_t = make_query_marks()

    @pl.loop(0, heads)
    def _(h):
        qt_ref[h, :HD] = q_ref[:, lanes(h)].astype(jnp.float32).T.astype(jnp.bfloat16)
        qt_ref[h, HD:] = marks_t

    @pl.loop(0, heads, step=2)
    def _(h0):
        @pl.loop(0, 2 * EARLY)
        def _(j):
            send_main(h0 * EARLY + j)

        def parts_of(h, half):
            rows = pl.ds(half * 2, TH - 2)
            keys = k_ref[rows, :, lanes(h)].reshape(OWN_SPAN, HD)
            return [(keys, own_marks[pl.ds(half * 2 * TW, OWN_SPAN)], v_ref[rows, :, lanes(h)].reshape(OWN_SPAN, HD))]

        absorb(h0, parts_of, first=True)

    west_marks[...] = key_marks(STRIP, strip_place(-R))
    east_marks[...] = key_marks(STRIP, strip_place(TW))
    north_marks[...] = key_marks(BAND, band_place(-R))
    south_marks[...] = key_marks(BAND, band_place(TH))

    def far_sources():
        slot = lax.broadcasted_iota(jnp.int32, (far_lists.shape[0], SLOTS), 1)
        found = [
            jnp.where(slot < CLOSE, first, jnp.where(slot < MAIN, second, third))
            for first, second, third in zip(close_offset(slot), edge_offset(slot - CLOSE), main_offset(slot - MAIN))
        ]
        source = tile_at(row, col, *(-part for part in found))
        return jnp.where(slot == UNUSED, -2, source[0] * COLS + source[1]).astype(jnp.float32)

    tile = lax.broadcasted_iota(jnp.int32, far_lists.shape, 1)
    own_list = jnp.max(jnp.where(tile == row * COLS + col, far_lists[...].astype(jnp.float32), -1.0), axis=1, keepdims=True)
    listed = jnp.max(jnp.where(far_sources() == own_list, 0.0, LOW).astype(jnp.float32), axis=0, keepdims=True)
    live_ref[...] = jnp.broadcast_to(listed, live_ref.shape).T

    @pl.loop(0, SLOTS // 2)
    def _(pair):
        both = [jnp.broadcast_to(live_ref[pl.ds(2 * pair + i, 1), :], (BLK, HD)) for i in (0, 1)]
        lane = lax.broadcasted_iota(jnp.int32, (2 * BLK, HD), 1)
        marks = jnp.where(lane == DEAD_AT, jnp.concatenate(both, axis=0), 0.0)
        far_marks[pl.ds(pl.multiple_of(pair * 2 * BLK, 2 * BLK), 2 * BLK)] = marks.astype(jnp.bfloat16)

    def use_far(group):
        first, count = GROUPS[group]
        regular = CLOSE + GROUPS[1][0] - MAIN if group == 0 else count
        part = far_ref.at[pl.ds(first, regular)]
        pltpu.make_async_remote_copy(
            src_ref=part, dst_ref=part, send_sem=far_send, recv_sem=far_recv.at[group],
            device_id=(row, (col + 1) % COLS), device_id_type=MESH,
        ).wait_recv()
        if group == 0:
            for i in range(len(EDGE)):
                _, _, receives, copy = edge(i)

                @pl.when(receives)
                def _(copy=copy):
                    copy.wait_recv()

        @pl.loop(first // 2, (first + count) // 2)
        def _(pair):
            rows = pl.ds(pl.multiple_of(pair * 2 * BLK, 2 * BLK), 2 * BLK)
            one, two = far_ref[2 * pair].astype(jnp.float32), far_ref[2 * pair + 1].astype(jnp.float32)
            far_k[rows] = jnp.concatenate([one[:BLK], two[:BLK]], axis=0).astype(jnp.bfloat16)
            far_v[rows] = jnp.concatenate([one[BLK:], two[BLK:]], axis=0).astype(jnp.bfloat16)

        @pl.loop(0, heads, step=2)
        def _(h0):
            rows = pl.ds(first * BLK, count * BLK)
            absorb(h0, lambda h, half: [(far_k[rows, lanes(h)], far_marks[rows], far_v[rows, lanes(h)])], halves=(None,))

    use_far(0)
    use_far(1)
    wait_halo(NORTH)
    wait_halo(SOUTH)
    for i, piece in enumerate((NW, NE, SW, SE)):
        @pl.when(jnp.logical_not(crossing[piece]))
        def _(i=i, piece=piece):
            for n, ref in enumerate((kn_ref, vn_ref) if piece in (NW, NE) else (ks_ref, vs_ref)):
                pack(ref, 0, R, piece in (NW, SW), corner_ref.at[2 * i + n])
        start_halo(piece)

    @pl.loop(heads * EARLY, heads * EARLY + LATE)
    def _(p):
        send_main(p)

    wait_halo(WEST)
    wait_halo(EAST)

    @pl.loop(0, heads, step=2)
    def _(h0):
        def parts_of(h, half):
            band_k, band_v, marks = ((kn_ref, vn_ref, north_marks), (ks_ref, vs_ref, south_marks))[half]
            found = [(band_k[:, :, lanes(h)].reshape(BAND, HD), marks[...], band_v[:, :, lanes(h)].reshape(BAND, HD))]
            for strip_k, strip_v, marks in ((kw_ref, vw_ref, west_marks), (ke_ref, ve_ref, east_marks)):
                found.append((strip_k[middle, lanes(h)], marks[middle], strip_v[middle, lanes(h)]))
            return found

        absorb(h0, parts_of)

    use_far(2)
    for piece in (NW, NE, SW, SE):
        wait_halo(piece)

    @pl.loop(0, heads, step=2)
    def _(h0):
        def parts_of(h, half):
            end = (top, bottom)[half]
            return [
                (strip_k[end, lanes(h)], marks[end], strip_v[end, lanes(h)])
                for strip_k, strip_v, marks in ((kw_ref, vw_ref, west_marks), (ke_ref, ve_ref, east_marks))
            ]

        absorb(h0, parts_of)

    use_far(3)

    @pl.loop(0, heads)
    def _(h):
        att_ref[:, lanes(h)] = (acc_ref[h] / l_ref[h]).T.astype(jnp.bfloat16)

    out_copy = pltpu.make_async_copy(att_ref, att_hbm, out_sem)
    out_copy.start()

    for piece in range(8):
        wait_halo_sent(piece)
        if piece in crossing:
            wait_halo_sent(piece, True)
    sent = stage_ref.at[pl.ds(0, CLOSE + N_MAIN)]
    pltpu.make_async_remote_copy(
        src_ref=sent, dst_ref=sent, send_sem=far_send, recv_sem=far_recv.at[0],
        device_id=(row, (col + 1) % COLS), device_id_type=MESH,
    ).wait_send()
    for i in range(len(EDGE)):
        _, sends, _, copy = edge(i)

        @pl.when(sends)
        def _(copy=copy):
            copy.wait_send()
    out_copy.wait()


def shards(
    queries, fresh_keys, fresh_values, stale_keys, stale_values, weight_out, gate, far_tiles, far_blocks, far_count
):
    inner = queries.shape[2]
    heads = inner // HD
    model = weight_out.shape[1]
    own = lax.axis_index("row") * COLS + lax.axis_index("col")
    block_of = jnp.sum(jnp.where(far_tiles == own, far_blocks, 0), axis=1)

    bf16, f32 = jnp.bfloat16, jnp.float32
    tokens = TH * TW
    any_spec = pl.BlockSpec(memory_space=pl.ANY)
    vmem_spec = pl.BlockSpec(memory_space=pltpu.VMEM)
    smem_spec = pl.BlockSpec(memory_space=pltpu.SMEM)
    band, strip = (R, TW, inner), (STRIP, inner)
    attended = pl.pallas_call(
        kernel,
        out_shape=jax.ShapeDtypeStruct((tokens, inner), bf16),
        in_specs=[any_spec] * 5 + [vmem_spec, smem_spec],
        out_specs=any_spec,
        scratch_shapes=[
            pltpu.VMEM((tokens, inner), bf16),
            pltpu.VMEM((TH, TW, inner), bf16),
            pltpu.VMEM((TH, TW, inner), bf16),
            pltpu.VMEM((tokens // 16, 16, inner), bf16),
            pltpu.VMEM((tokens // 16, 16, inner), bf16),
            pltpu.VMEM(band, bf16), pltpu.VMEM(band, bf16), pltpu.VMEM(strip, bf16), pltpu.VMEM(strip, bf16),
            pltpu.VMEM(band, bf16), pltpu.VMEM(band, bf16), pltpu.VMEM(strip, bf16), pltpu.VMEM(strip, bf16),
            pltpu.VMEM((SIDE, inner), f32),
            pltpu.VMEM((4, SIDE, inner), bf16),
            pltpu.VMEM((8, CORNER, inner), bf16),
            pltpu.VMEM((SLOTS, 2 * BLK, inner), bf16),
            pltpu.VMEM((SLOTS, 2 * BLK, inner), bf16),
            pltpu.VMEM((heads, HD, tokens), f32),
            pltpu.VMEM((heads, 1, tokens), f32),
            pltpu.VMEM((heads, 1, tokens), f32),
            pltpu.VMEM((heads, 2 * HD, tokens), bf16),
            pltpu.VMEM((SLOTS * BLK, inner), bf16),
            pltpu.VMEM((SLOTS * BLK, inner), bf16),
            pltpu.VMEM((tokens, HD), bf16),
            pltpu.VMEM((BAND, HD), bf16),
            pltpu.VMEM((BAND, HD), bf16),
            pltpu.VMEM((STRIP, HD), bf16),
            pltpu.VMEM((STRIP, HD), bf16),
            pltpu.VMEM((SLOTS * BLK, HD), bf16),
            pltpu.VMEM((SLOTS, 128), f32),
            pltpu.VMEM((tokens, inner), bf16),
            pltpu.SemaphoreType.DMA((5,)),
            pltpu.SemaphoreType.DMA((16,)),
            pltpu.SemaphoreType.DMA((16,)),
            pltpu.SemaphoreType.DMA,
            pltpu.SemaphoreType.DMA((len(GROUPS),)),
            pltpu.SemaphoreType.DMA((len(EDGE),)),
            pltpu.SemaphoreType.DMA((len(EDGE),)),
            pltpu.SemaphoreType.DMA,
        ],
        compiler_params=pltpu.CompilerParams(has_side_effects=True, vmem_limit_bytes=52 * 1024 * 1024),
        name="attention",
    )(
        queries.reshape(tokens, inner), fresh_keys, fresh_values,
        stale_keys.reshape(-1, 16, inner), stale_values.reshape(-1, 16, inner), far_tiles.T, block_of,
    )
    projected = jnp.dot(attended, weight_out, preferred_element_type=jnp.float32)
    return (projected * gate[None, :]).astype(bf16).reshape(TH, TW, model)


def solution(mesh):
    tile = P("row", "col", None)
    return jax.shard_map(
        shards, mesh=mesh, in_specs=(tile,) * 5 + (P(),) * 5, out_specs=tile, check_vma=False,
    )
```

```python
import jax
import jax.numpy as jnp
from jax import lax
from jax.experimental import pallas as pl
from jax.experimental.pallas import tpu as pltpu
from jax.sharding import PartitionSpec as P

HD = 128
R = 6
BLK = 8
ROWS = 8
COLS = 16
TH = 16
TW = 32
HALF = 256
LOW = -1e30
SCALE = HD ** (-0.5) * 1.4426950408889634
MESH = pl.DeviceIdType.MESH

CLOSE = 29
EDGE = [(i, f, e) for i in (-1, 0, 1) for f in (0, 1) for e in (-1, 1)] + [(-1, 0, 0), (1, 0, 0)]
UNUSED = CLOSE + len(EDGE)
MAIN = UNUSED + 1
MIX = 25
SLOTS = 128
N_MAIN = SLOTS - MAIN
MID = COLS // 2
GROUPS = ((0, 48), (48, 32), (80, 32), (112, 16))
EARLY = 4


def blend(late, before, after):
    return before + late * (after - before)


def close_offset(j):
    dr = blend(j // 24, 2 + 2 * (j % 3), 0)
    e = blend(j // 24, j // 3, j - 22)
    return dr, 0, e


def edge_offset(i):
    last = i // 12
    return blend(last, i // 4 - 1, 2 * (i - 12) - 1), blend(last, i // 2 % 2, 0), blend(last, 2 * (i % 2) - 1, 0)


def main_offset(p):
    i = MIX * p % N_MAIN
    straight = i // 58
    k = i - 40
    e1 = blend(i // 40, i // 5, k // 3 + (k // 3 + 5) // 6)
    dr1 = blend(i // 40, 2 + i % 5, 7 + k % 3)
    k = i - 58
    e2 = blend(i // 74, k // 2, 2 + (k - 16) // 2)
    dr2 = blend(i // 74, 3 + 2 * (k % 2), 7 + 2 * (k % 2))
    return blend(straight, dr1, dr2), 1 - straight, blend(straight, e1, e2)


def tile_at(row, col, dr, f, e):
    return (row + dr + 2 * ROWS) % ROWS, (col // MID + f + 2) % 2 * MID + (col % MID + e + 2 * MID) % MID


ROW_AT, COL_AT, PAD_AT, DEAD_AT = 0, TH + 2 * R, TH + TW + 4 * R, TH + TW + 4 * R + 1

NORTH, SOUTH, WEST, EAST, NW, NE, SW, SE = range(8)
BAND = R * TW
CORNER = 48
SIDE = TH * R
STRIP = SIDE + 2 * CORNER
OWN_SPAN = (TH - 2) * TW


def kernel(
    q_hbm, k_hbm, v_hbm, sk_hbm, sv_hbm, far_lists, block_of, att_hbm,
    q_ref, k_ref, v_ref, sk_ref, sv_ref,
    kn_ref, ks_ref, kw_ref, ke_ref, vn_ref, vs_ref, vw_ref, ve_ref,
    pack_ref, side_ref, corner_ref,
    far_ref, stage_ref, acc_ref, m_ref, l_ref, qt_ref, far_k, far_v, own_marks, north_marks, south_marks, west_marks, east_marks, far_marks,
    live_ref, att_ref,
    load_sem, halo_send, halo_recv, far_send, far_recv, edge_send, edge_recv, out_sem,
):
    heads = q_ref.shape[1] // HD
    row = lax.axis_index("row")
    col = lax.axis_index("col")
    has_n, has_s = row > 0, row < ROWS - 1
    has_w, has_e = col > 0, col < COLS - 1
    exists = {
        NORTH: has_n, SOUTH: has_s, WEST: has_w, EAST: has_e,
        NW: has_n & has_w, NE: has_n & has_e, SW: has_s & has_w, SE: has_s & has_e,
    }

    crossing = {NW: col == MID - 1, SW: col == MID - 1, NE: col == MID, SE: col == MID}

    def halo_copies(piece, straight=False):
        up, down = (row - 1 + ROWS) % ROWS, (row + 1) % ROWS
        left, right = (col - 1 + COLS) % COLS, (col + 1) % COLS
        lower, upper = pl.ds(TH - R, R), pl.ds(0, R)
        top, middle, bottom = pl.ds(0, CORNER), pl.ds(CORNER, SIDE), pl.ds(CORNER + SIDE, CORNER)
        plan = {
            NORTH: (has_s, (down, col), (k_hbm.at[lower], v_hbm.at[lower]), (kn_ref, vn_ref)),
            SOUTH: (has_n, (up, col), (k_hbm.at[upper], v_hbm.at[upper]), (ks_ref, vs_ref)),
            WEST: (has_e, (row, right), (side_ref.at[0], side_ref.at[1]), (kw_ref.at[middle], vw_ref.at[middle])),
            EAST: (has_w, (row, left), (side_ref.at[2], side_ref.at[3]), (ke_ref.at[middle], ve_ref.at[middle])),
            NW: (has_n & has_e, (row, right), (corner_ref.at[0], corner_ref.at[1]), (kw_ref.at[top], vw_ref.at[top])),
            NE: (has_n & has_w, (row, left), (corner_ref.at[2], corner_ref.at[3]), (ke_ref.at[top], ve_ref.at[top])),
            SW: (has_s & has_e, (row, right), (corner_ref.at[4], corner_ref.at[5]),
                 (kw_ref.at[bottom], vw_ref.at[bottom])),
            SE: (has_s & has_w, (row, left), (corner_ref.at[6], corner_ref.at[7]),
                 (ke_ref.at[bottom], ve_ref.at[bottom])),
        }
        sends, target, srcs, dsts = plan[piece]
        if piece in crossing:
            if straight:
                sends = crossing[piece] & (has_s if piece in (NW, NE) else has_n)
                target = (down if piece in (NW, NE) else up, target[1])
            else:
                sends = sends & jnp.logical_not(crossing[piece])
        copies = [
            pltpu.make_async_remote_copy(
                src_ref=src, dst_ref=dst,
                send_sem=halo_send.at[2 * piece + i], recv_sem=halo_recv.at[2 * piece + i],
                device_id=target, device_id_type=MESH,
            )
            for i, (src, dst) in enumerate(zip(srcs, dsts))
        ]
        return sends, copies

    def start_halo(piece, straight=False):
        sends, copies = halo_copies(piece, straight)

        @pl.when(sends)
        def _():
            for copy in copies:
                copy.start()

    def wait_halo(piece):
        _, copies = halo_copies(piece)

        @pl.when(exists[piece])
        def _():
            for copy in copies:
                copy.wait_recv()

    def wait_halo_sent(piece, straight=False):
        sends, copies = halo_copies(piece, straight)

        @pl.when(sends)
        def _():
            for copy in copies:
                copy.wait_send()

    start_halo(NORTH)
    start_halo(SOUTH)

    loads = [
        pltpu.make_async_copy(src, dst, load_sem.at[i])
        for i, (src, dst) in enumerate(
            ((sk_hbm, sk_ref), (sv_hbm, sv_ref), (k_hbm, k_ref), (v_hbm, v_ref), (q_hbm, q_ref))
        )
    ]
    for load in loads:
        load.start()

    def far_copy(slot, target, send_sem, recv_sem):
        return pltpu.make_async_remote_copy(
            src_ref=stage_ref.at[slot], dst_ref=far_ref.at[slot], send_sem=send_sem, recv_sem=recv_sem,
            device_id=target, device_id_type=MESH,
        )

    def fill(slot, target):
        block = block_of[target[0] * COLS + target[1]]
        pair, odd = lax.shift_right_logical(block, 1), block & 1
        both = []
        for ref in (sk_ref, sv_ref):
            rows = ref[pair].astype(jnp.float32)
            both.append(jnp.where(odd == 1, rows[BLK:], rows[:BLK]))
        stage_ref[slot] = jnp.concatenate(both, axis=0).astype(jnp.bfloat16)

    def send_far(slot, offset, sem):
        target = tile_at(row, col, *offset)
        fill(slot, target)
        far_copy(slot, target, far_send, far_recv.at[sem]).start()

    loads[0].wait()
    loads[1].wait()

    @pl.loop(0, CLOSE)
    def _(j):
        send_far(j, close_offset(j), 0)

    def send_main(p):
        send_far(MAIN + p, main_offset(p), (MAIN + p - 16) // 32)

    for p in range(EARLY):
        send_main(p)

    def touches(dr, other):
        return (row + dr >= 0) & (row + dr < ROWS) & (other[1] - col >= -1) & (other[1] - col <= 1)

    def edge(i):
        dr, f, e = EDGE[i]
        target, origin = tile_at(row, col, dr, f, e), tile_at(row, col, -dr, -f, -e)
        copy = far_copy(CLOSE + i, target, edge_send.at[i], edge_recv.at[i])
        return target, jnp.logical_not(touches(dr, target)), jnp.logical_not(touches(-dr, origin)), copy

    for i in range(len(EDGE)):
        target, sends, receives, copy = edge(i)

        @pl.when(sends)
        def _(i=i, target=target, copy=copy):
            fill(CLOSE + i, target)
            copy.start()

        @pl.when(jnp.logical_not(receives))
        def _(i=i):
            far_ref[CLOSE + i] = jnp.zeros(far_ref.shape[1:], far_ref.dtype)

    far_ref[UNUSED] = jnp.zeros(far_ref.shape[1:], far_ref.dtype)

    def pack(source, first, count, right, target):
        for r in range(count):
            if right:
                edge = source[first + r, TW - 16:].astype(jnp.float32)[16 - R:]
            else:
                edge = source[first + r, :16].astype(jnp.float32)[:R]
            pack_ref[pl.ds(r * R, R)] = edge
        if target.shape[0] > count * R:
            pack_ref[count * R:target.shape[0]] = jnp.zeros((target.shape[0] - count * R, pack_ref.shape[1]), jnp.float32)
        target[...] = pack_ref[:target.shape[0]].astype(jnp.bfloat16)

    loads[2].wait()
    loads[3].wait()
    for i, (ref, right) in enumerate(((k_ref, True), (v_ref, True), (k_ref, False), (v_ref, False))):
        pack(ref, 0, TH, right, side_ref.at[i])
    start_halo(WEST)
    start_halo(EAST)
    for i, piece in enumerate((NW, NE, SW, SE)):
        @pl.when(crossing[piece])
        def _(i=i, piece=piece):
            for n, ref in enumerate((k_ref, v_ref)):
                pack(ref, TH - R if piece in (NW, NE) else 0, R, piece in (NW, SW), corner_ref.at[2 * i + n])
        start_halo(piece, True)

    def clear(missing, refs):
        @pl.when(missing)
        def _():
            for ref in refs:
                ref[...] = jnp.zeros(ref.shape, ref.dtype)

    top, middle, bottom = pl.ds(0, CORNER), pl.ds(CORNER, SIDE), pl.ds(CORNER + SIDE, CORNER)
    clear(jnp.logical_not(has_n), [kn_ref, vn_ref])
    clear(jnp.logical_not(has_s), [ks_ref, vs_ref])
    clear(jnp.logical_not(has_w), [kw_ref.at[middle], vw_ref.at[middle]])
    clear(jnp.logical_not(has_e), [ke_ref.at[middle], ve_ref.at[middle]])
    clear(jnp.logical_not(exists[NW]), [kw_ref.at[top], vw_ref.at[top]])
    clear(jnp.logical_not(exists[SW]), [kw_ref.at[bottom], vw_ref.at[bottom]])
    clear(jnp.logical_not(exists[NE]), [ke_ref.at[top], ve_ref.at[top]])
    clear(jnp.logical_not(exists[SE]), [ke_ref.at[bottom], ve_ref.at[bottom]])

    def key_marks(shape, place):
        u, v, real = place(shape)
        lane = lax.broadcasted_iota(jnp.int32, shape, len(shape) - 1)
        on = (lane == u + R + ROW_AT) | (lane == v + R + COL_AT) | ((lane == PAD_AT) & jnp.logical_not(real))
        return jnp.where(on, 1.0, 0.0).reshape(-1, HD).astype(jnp.bfloat16)

    def make_query_marks():
        shape = (HD, TH * TW)
        lane = lax.broadcasted_iota(jnp.int32, shape, 0)
        query = lax.broadcasted_iota(jnp.int32, (1, TH * TW), 1)
        query_row, query_col = query // TW, query % TW
        u, v = lane - ROW_AT - R, lane - COL_AT - R
        row_off = (jnp.abs(u - query_row) > R) | (u + row * TH < 0) | (u + row * TH >= ROWS * TH)
        col_off = (jnp.abs(v - query_col) > R) | (v + col * TW < 0) | (v + col * TW >= COLS * TW)
        low = ((lane < COL_AT) & row_off) | ((lane >= COL_AT) & (lane < PAD_AT) & col_off) | (lane == PAD_AT)
        return jnp.where(low, LOW, jnp.where(lane == DEAD_AT, 1.0, 0.0)).astype(jnp.bfloat16)

    def strip_place(first_col):
        def place(shape):
            key = lax.broadcasted_iota(jnp.int32, shape, 0)
            upper, lower = key < CORNER, key >= CORNER + SIDE
            start = jnp.where(upper, 0, jnp.where(lower, CORNER + SIDE, CORNER))
            first_row = jnp.where(upper, -R, jnp.where(lower, TH, 0))
            cell = key - start
            real = (cell < R * R) | jnp.logical_not(upper | lower)
            return first_row + cell // R, first_col + cell % R, real

        return place

    def band_place(first_row):
        def place(shape):
            u, v = (lax.broadcasted_iota(jnp.int32, shape, axis) for axis in (0, 1))
            return first_row + u, v, v >= 0

        return place

    own_marks[...] = key_marks((TH, TW, HD), band_place(0))

    def lanes(h):
        return pl.ds(pl.multiple_of(h * HD, HD), HD)

    def across(half):
        return pl.ds(0, 2 * HALF) if half is None else pl.ds(half * HALF, HALF)

    def scores(keys, query):
        return jnp.dot(keys, query, preferred_element_type=jnp.float32)

    def mix(values, weights):
        return lax.dot_general(values, weights, (((0,), (0,)), ((), ())), preferred_element_type=jnp.float32)

    def absorb(h0, parts_of, first=False, halves=(0, 1), last=False):
        chains = [(h0 + i, half) for i in (0, 1) for half in halves]

        def start(chain):
            h, half = chain
            query = qt_ref[h, :, across(half)]
            parts = parts_of(h, half)
            return [(scores(jnp.concatenate([keys, marks], axis=1), query), values) for keys, marks, values in parts]

        def finish(chain, parts):
            h, half = chain
            peak = jnp.max(parts[0][0], axis=0, keepdims=True)
            for raw, _ in parts[1:]:
                peak = jnp.maximum(peak, jnp.max(raw, axis=0, keepdims=True))
            if not first:
                before = m_ref[h, :, across(half)]
                peak = jnp.maximum(before, peak)
            total, mixed = None, None
            for raw, values in parts:
                weights = jnp.exp2((raw - peak) * SCALE)
                part = jnp.sum(weights, axis=0, keepdims=True)
                product = mix(values, weights.astype(jnp.bfloat16))
                total = part if total is None else total + part
                mixed = product if mixed is None else mixed + product
            if not first:
                fade = jnp.exp2((before - peak) * SCALE)
                total = l_ref[h, :, across(half)] * fade + total
                mixed = acc_ref[h, :, across(half)] * fade + mixed
            return peak, total, mixed

        results = []
        ready = start(chains[0])
        for n, chain in enumerate(chains):
            parts = ready
            if n + 1 < len(chains):
                ready = start(chains[n + 1])
            results.append(finish(chain, parts))
        if last:
            for (h, half), (_, total, mixed) in zip(chains, results):
                att_ref[across(half), lanes(h)] = (mixed / total).T.astype(jnp.bfloat16)
            return
        for (h, half), found in zip(chains, results):
            m_ref[h, :, across(half)], l_ref[h, :, across(half)], acc_ref[h, :, across(half)] = found

    loads[4].wait()
    marks_t = make_query_marks()

    @pl.loop(0, heads)
    def _(h):
        qt_ref[h, :HD] = q_ref[:, lanes(h)].astype(jnp.float32).T.astype(jnp.bfloat16)
        qt_ref[h, HD:] = marks_t

    @pl.loop(0, heads, step=2)
    def _(h0):
        def parts_of(h, half):
            rows = pl.ds(half * 2, TH - 2)
            keys = k_ref[rows, :, lanes(h)].reshape(OWN_SPAN, HD)
            return [(keys, own_marks[pl.ds(half * 2 * TW, OWN_SPAN)], v_ref[rows, :, lanes(h)].reshape(OWN_SPAN, HD))]

        absorb(h0, parts_of, first=True)

    west_marks[...] = key_marks((STRIP, HD), strip_place(-R))
    east_marks[...] = key_marks((STRIP, HD), strip_place(TW))
    north_marks[...] = key_marks((R, TW, HD), band_place(-R))
    south_marks[...] = key_marks((R, TW, HD), band_place(TH))

    def far_sources():
        slot = lax.broadcasted_iota(jnp.int32, (1, SLOTS), 1)
        found = [
            jnp.where(slot < CLOSE, first, jnp.where(slot < MAIN, second, third))
            for first, second, third in zip(close_offset(slot), edge_offset(slot - CLOSE), main_offset(slot - MAIN))
        ]
        source = tile_at(row, col, *(-part for part in found))
        return jnp.where(slot == UNUSED, -2, source[0] * COLS + source[1]).astype(jnp.float32)

    tile = lax.broadcasted_iota(jnp.int32, far_lists.shape, 1)
    own_list = jnp.max(jnp.where(tile == row * COLS + col, far_lists[...].astype(jnp.float32), -1.0), axis=1, keepdims=True)
    listed = jnp.max(jnp.where(far_sources() == own_list, 0.0, LOW).astype(jnp.float32), axis=0, keepdims=True)
    live_ref[...] = jnp.broadcast_to(listed, live_ref.shape).T

    @pl.loop(0, SLOTS // 2)
    def _(pair):
        both = [jnp.broadcast_to(live_ref[pl.ds(2 * pair + i, 1), :], (BLK, HD)) for i in (0, 1)]
        lane = lax.broadcasted_iota(jnp.int32, (2 * BLK, HD), 1)
        marks = jnp.where(lane == DEAD_AT, jnp.concatenate(both, axis=0), 0.0)
        far_marks[pl.ds(pl.multiple_of(pair * 2 * BLK, 2 * BLK), 2 * BLK)] = marks.astype(jnp.bfloat16)

    def use_far(group):
        first, count = GROUPS[group]
        regular = CLOSE + GROUPS[1][0] - MAIN if group == 0 else count
        part = far_ref.at[pl.ds(first, regular)]
        pltpu.make_async_remote_copy(
            src_ref=part, dst_ref=part, send_sem=far_send, recv_sem=far_recv.at[group],
            device_id=(row, (col + 1) % COLS), device_id_type=MESH,
        ).wait_recv()
        if group == 0:
            for i in range(len(EDGE)):
                _, _, receives, copy = edge(i)

                @pl.when(receives)
                def _(copy=copy):
                    copy.wait_recv()

        @pl.loop(first // 2, (first + count) // 2)
        def _(pair):
            rows = pl.ds(pl.multiple_of(pair * 2 * BLK, 2 * BLK), 2 * BLK)
            one, two = far_ref[2 * pair].astype(jnp.float32), far_ref[2 * pair + 1].astype(jnp.float32)
            far_k[rows] = jnp.concatenate([one[:BLK], two[:BLK]], axis=0).astype(jnp.bfloat16)
            far_v[rows] = jnp.concatenate([one[BLK:], two[BLK:]], axis=0).astype(jnp.bfloat16)

        @pl.loop(0, heads, step=2)
        def _(h0):
            rows = pl.ds(first * BLK, count * BLK)
            absorb(h0, lambda h, half: [(far_k[rows, lanes(h)], far_marks[rows], far_v[rows, lanes(h)])],
                   halves=(None,), last=group == len(GROUPS) - 1)

    use_far(0)
    wait_halo(NORTH)
    wait_halo(SOUTH)
    for i, piece in enumerate((NW, NE, SW, SE)):
        @pl.when(jnp.logical_not(crossing[piece]))
        def _(i=i, piece=piece):
            for n, ref in enumerate((kn_ref, vn_ref) if piece in (NW, NE) else (ks_ref, vs_ref)):
                pack(ref, 0, R, piece in (NW, SW), corner_ref.at[2 * i + n])
        start_halo(piece)

    @pl.loop(EARLY, N_MAIN)
    def _(p):
        send_main(p)

    wait_halo(WEST)
    wait_halo(EAST)

    @pl.loop(0, heads, step=2)
    def _(h0):
        def parts_of(h, half):
            band_k, band_v, marks = ((kn_ref, vn_ref, north_marks), (ks_ref, vs_ref, south_marks))[half]
            found = [(band_k[:, :, lanes(h)].reshape(BAND, HD), marks[...], band_v[:, :, lanes(h)].reshape(BAND, HD))]
            for strip_k, strip_v, marks in ((kw_ref, vw_ref, west_marks), (ke_ref, ve_ref, east_marks)):
                found.append((strip_k[middle, lanes(h)], marks[middle], strip_v[middle, lanes(h)]))
            return found

        absorb(h0, parts_of)

    use_far(1)
    use_far(2)
    for piece in (NW, NE, SW, SE):
        wait_halo(piece)

    @pl.loop(0, heads, step=2)
    def _(h0):
        def parts_of(h, half):
            end = (top, bottom)[half]
            return [
                (strip_k[end, lanes(h)], marks[end], strip_v[end, lanes(h)])
                for strip_k, strip_v, marks in ((kw_ref, vw_ref, west_marks), (ke_ref, ve_ref, east_marks))
            ]

        absorb(h0, parts_of)

    use_far(3)

    out_copy = pltpu.make_async_copy(att_ref, att_hbm, out_sem)
    out_copy.start()

    for piece in range(8):
        wait_halo_sent(piece)
        if piece in crossing:
            wait_halo_sent(piece, True)
    sent = stage_ref.at[pl.ds(0, CLOSE + N_MAIN)]
    pltpu.make_async_remote_copy(
        src_ref=sent, dst_ref=sent, send_sem=far_send, recv_sem=far_recv.at[0],
        device_id=(row, (col + 1) % COLS), device_id_type=MESH,
    ).wait_send()
    for i in range(len(EDGE)):
        _, sends, _, copy = edge(i)

        @pl.when(sends)
        def _(copy=copy):
            copy.wait_send()
    out_copy.wait()


def shards(
    queries, fresh_keys, fresh_values, stale_keys, stale_values, weight_out, gate, far_tiles, far_blocks, far_count
):
    inner = queries.shape[2]
    heads = inner // HD
    model = weight_out.shape[1]
    own = lax.axis_index("row") * COLS + lax.axis_index("col")
    block_of = jnp.sum(jnp.where(far_tiles == own, far_blocks, 0), axis=1)

    bf16, f32 = jnp.bfloat16, jnp.float32
    tokens = TH * TW
    any_spec = pl.BlockSpec(memory_space=pl.ANY)
    vmem_spec = pl.BlockSpec(memory_space=pltpu.VMEM)
    smem_spec = pl.BlockSpec(memory_space=pltpu.SMEM)
    band, strip = (R, TW, inner), (STRIP, inner)
    attended = pl.pallas_call(
        kernel,
        out_shape=jax.ShapeDtypeStruct((tokens, inner), bf16),
        in_specs=[any_spec] * 5 + [vmem_spec, smem_spec],
        out_specs=any_spec,
        scratch_shapes=[
            pltpu.VMEM((tokens, inner), bf16),
            pltpu.VMEM((TH, TW, inner), bf16),
            pltpu.VMEM((TH, TW, inner), bf16),
            pltpu.VMEM((tokens // 16, 16, inner), bf16),
            pltpu.VMEM((tokens // 16, 16, inner), bf16),
            pltpu.VMEM(band, bf16), pltpu.VMEM(band, bf16), pltpu.VMEM(strip, bf16), pltpu.VMEM(strip, bf16),
            pltpu.VMEM(band, bf16), pltpu.VMEM(band, bf16), pltpu.VMEM(strip, bf16), pltpu.VMEM(strip, bf16),
            pltpu.VMEM((SIDE, inner), f32),
            pltpu.VMEM((4, SIDE, inner), bf16),
            pltpu.VMEM((8, CORNER, inner), bf16),
            pltpu.VMEM((SLOTS, 2 * BLK, inner), bf16),
            pltpu.VMEM((SLOTS, 2 * BLK, inner), bf16),
            pltpu.VMEM((heads, HD, tokens), f32),
            pltpu.VMEM((heads, 1, tokens), f32),
            pltpu.VMEM((heads, 1, tokens), f32),
            pltpu.VMEM((heads, 2 * HD, tokens), bf16),
            pltpu.VMEM((SLOTS * BLK, inner), bf16),
            pltpu.VMEM((SLOTS * BLK, inner), bf16),
            pltpu.VMEM((tokens, HD), bf16),
            pltpu.VMEM((BAND, HD), bf16),
            pltpu.VMEM((BAND, HD), bf16),
            pltpu.VMEM((STRIP, HD), bf16),
            pltpu.VMEM((STRIP, HD), bf16),
            pltpu.VMEM((SLOTS * BLK, HD), bf16),
            pltpu.VMEM((SLOTS, 128), f32),
            pltpu.VMEM((tokens, inner), bf16),
            pltpu.SemaphoreType.DMA((5,)),
            pltpu.SemaphoreType.DMA((16,)),
            pltpu.SemaphoreType.DMA((16,)),
            pltpu.SemaphoreType.DMA,
            pltpu.SemaphoreType.DMA((len(GROUPS),)),
            pltpu.SemaphoreType.DMA((len(EDGE),)),
            pltpu.SemaphoreType.DMA((len(EDGE),)),
            pltpu.SemaphoreType.DMA,
        ],
        compiler_params=pltpu.CompilerParams(has_side_effects=True, vmem_limit_bytes=52 * 1024 * 1024),
        name="attention",
    )(
        queries.reshape(tokens, inner), fresh_keys, fresh_values,
        stale_keys.reshape(-1, 16, inner), stale_values.reshape(-1, 16, inner), far_tiles.T, block_of,
    )
    projected = jnp.dot(attended, weight_out, preferred_element_type=jnp.float32)
    return (projected * gate[None, :]).astype(bf16).reshape(TH, TW, model)


def solution(mesh):
    tile = P("row", "col", None)
    return jax.shard_map(
        shards, mesh=mesh, in_specs=(tile,) * 5 + (P(),) * 5, out_specs=tile, check_vma=False,
    )
```

```python
import jax
import jax.numpy as jnp
from jax import lax
from jax.experimental import pallas as pl
from jax.experimental.pallas import tpu as pltpu
from jax.sharding import PartitionSpec as P

HD = 128
R = 6
BLK = 8
ROWS = 8
COLS = 16
TH = 16
TW = 32
HALF = 256
LOW = -1e30
SCALE = HD ** (-0.5) * 1.4426950408889634
MESH = pl.DeviceIdType.MESH

CLOSE = 29
EDGE = [(i, f, e) for i in (-1, 0, 1) for f in (0, 1) for e in (-1, 1)] + [(-1, 0, 0), (1, 0, 0)]
UNUSED = CLOSE + len(EDGE)
MAIN = UNUSED + 1
MIX = 25
SLOTS = 128
N_MAIN = SLOTS - MAIN
MID = COLS // 2
GROUPS = ((0, MAIN), (MAIN, 32), (76, 32), (108, 20))
AHEAD = 5


def blend(late, before, after):
    return before + late * (after - before)


def close_offset(j):
    dr = blend(j // 24, 2 + 2 * (j % 3), 0)
    e = blend(j // 24, j // 3, j - 22)
    return dr, 0, e


def edge_offset(i):
    last = i // 12
    return blend(last, i // 4 - 1, 2 * (i - 12) - 1), blend(last, i // 2 % 2, 0), blend(last, 2 * (i % 2) - 1, 0)


def main_offset(p):
    i = MIX * p % N_MAIN
    straight = i // 58
    k = i - 40
    e1 = blend(i // 40, i // 5, k // 3 + (k // 3 + 5) // 6)
    dr1 = blend(i // 40, 2 + i % 5, 7 + k % 3)
    k = i - 58
    e2 = blend(i // 74, k // 2, 2 + (k - 16) // 2)
    dr2 = blend(i // 74, 3 + 2 * (k % 2), 7 + 2 * (k % 2))
    return blend(straight, dr1, dr2), 1 - straight, blend(straight, e1, e2)


def tile_at(row, col, dr, f, e):
    return (row + dr + 2 * ROWS) % ROWS, (col // MID + f + 2) % 2 * MID + (col % MID + e + 2 * MID) % MID


ROW_AT, COL_AT, PAD_AT, DEAD_AT = 0, TH + 2 * R, TH + TW + 4 * R, TH + TW + 4 * R + 1

NORTH, SOUTH, WEST, EAST, NW, NE, SW, SE = range(8)
BAND = R * TW
CORNER = 48
SIDE = TH * R
STRIP = SIDE + 2 * CORNER
OWN_SPAN = (TH - 2) * TW


def kernel(
    q_hbm, k_hbm, v_hbm, sk_hbm, sv_hbm, far_lists, block_of, att_hbm,
    q_ref, k_ref, v_ref, sk_ref, sv_ref,
    kn_ref, ks_ref, kw_ref, ke_ref, vn_ref, vs_ref, vw_ref, ve_ref,
    pack_ref, side_ref, corner_ref,
    far_ref, stage_ref, acc_ref, m_ref, l_ref, qt_ref, far_k, far_v, own_marks, north_marks, south_marks, west_marks, east_marks, far_marks,
    live_ref, att_ref,
    load_sem, halo_send, halo_recv, far_send, far_recv, edge_send, edge_recv, out_sem,
):
    heads = q_ref.shape[1] // HD
    row = lax.axis_index("row")
    col = lax.axis_index("col")
    has_n, has_s = row > 0, row < ROWS - 1
    has_w, has_e = col > 0, col < COLS - 1
    exists = {
        NORTH: has_n, SOUTH: has_s, WEST: has_w, EAST: has_e,
        NW: has_n & has_w, NE: has_n & has_e, SW: has_s & has_w, SE: has_s & has_e,
    }

    crossing = {NW: col == MID - 1, SW: col == MID - 1, NE: col == MID, SE: col == MID}

    def halo_copies(piece, straight=False):
        up, down = (row - 1 + ROWS) % ROWS, (row + 1) % ROWS
        left, right = (col - 1 + COLS) % COLS, (col + 1) % COLS
        lower, upper = pl.ds(TH - R, R), pl.ds(0, R)
        top, middle, bottom = pl.ds(0, CORNER), pl.ds(CORNER, SIDE), pl.ds(CORNER + SIDE, CORNER)
        plan = {
            NORTH: (has_s, (down, col), (k_hbm.at[lower], v_hbm.at[lower]), (kn_ref, vn_ref)),
            SOUTH: (has_n, (up, col), (k_hbm.at[upper], v_hbm.at[upper]), (ks_ref, vs_ref)),
            WEST: (has_e, (row, right), (side_ref.at[0], side_ref.at[1]), (kw_ref.at[middle], vw_ref.at[middle])),
            EAST: (has_w, (row, left), (side_ref.at[2], side_ref.at[3]), (ke_ref.at[middle], ve_ref.at[middle])),
            NW: (has_n & has_e, (row, right), (corner_ref.at[0], corner_ref.at[1]), (kw_ref.at[top], vw_ref.at[top])),
            NE: (has_n & has_w, (row, left), (corner_ref.at[2], corner_ref.at[3]), (ke_ref.at[top], ve_ref.at[top])),
            SW: (has_s & has_e, (row, right), (corner_ref.at[4], corner_ref.at[5]),
                 (kw_ref.at[bottom], vw_ref.at[bottom])),
            SE: (has_s & has_w, (row, left), (corner_ref.at[6], corner_ref.at[7]),
                 (ke_ref.at[bottom], ve_ref.at[bottom])),
        }
        sends, target, srcs, dsts = plan[piece]
        if piece in crossing:
            if straight:
                sends = crossing[piece] & (has_s if piece in (NW, NE) else has_n)
                target = (down if piece in (NW, NE) else up, target[1])
            else:
                sends = sends & jnp.logical_not(crossing[piece])
        copies = [
            pltpu.make_async_remote_copy(
                src_ref=src, dst_ref=dst,
                send_sem=halo_send.at[2 * piece + i], recv_sem=halo_recv.at[2 * piece + i],
                device_id=target, device_id_type=MESH,
            )
            for i, (src, dst) in enumerate(zip(srcs, dsts))
        ]
        return sends, copies

    def start_halo(piece, straight=False):
        sends, copies = halo_copies(piece, straight)

        @pl.when(sends)
        def _():
            for copy in copies:
                copy.start()

    def wait_halo(piece):
        _, copies = halo_copies(piece)

        @pl.when(exists[piece])
        def _():
            for copy in copies:
                copy.wait_recv()

    def wait_halo_sent(piece, straight=False):
        sends, copies = halo_copies(piece, straight)

        @pl.when(sends)
        def _():
            for copy in copies:
                copy.wait_send()

    start_halo(NORTH)
    start_halo(SOUTH)

    loads = [
        pltpu.make_async_copy(src, dst, load_sem.at[i])
        for i, (src, dst) in enumerate(
            ((sk_hbm, sk_ref), (sv_hbm, sv_ref), (k_hbm, k_ref), (v_hbm, v_ref), (q_hbm, q_ref))
        )
    ]
    for load in loads:
        load.start()

    def far_copy(slot, target, send_sem, recv_sem):
        return pltpu.make_async_remote_copy(
            src_ref=stage_ref.at[slot], dst_ref=far_ref.at[slot], send_sem=send_sem, recv_sem=recv_sem,
            device_id=target, device_id_type=MESH,
        )

    def fill(slot, target):
        block = block_of[target[0] * COLS + target[1]]
        pair, odd = lax.shift_right_logical(block, 1), block & 1
        both = []
        for ref in (sk_ref, sv_ref):
            rows = ref[pair].astype(jnp.float32)
            both.append(jnp.where(odd == 1, rows[BLK:], rows[:BLK]))
        stage_ref[slot] = jnp.concatenate(both, axis=0).astype(jnp.bfloat16)

    def send_far(slot, offset, sem):
        target = tile_at(row, col, *offset)
        fill(slot, target)
        far_copy(slot, target, far_send, far_recv.at[sem]).start()

    loads[0].wait()
    loads[1].wait()

    @pl.loop(0, AHEAD)
    def _(j):
        send_far(j, close_offset(j), 0)

    def send_main(p):
        send_far(MAIN + p, main_offset(p), 1 + p // 32)

    def touches(dr, other):
        return (row + dr >= 0) & (row + dr < ROWS) & (other[1] - col >= -1) & (other[1] - col <= 1)

    def edge(i):
        dr, f, e = EDGE[i]
        target, origin = tile_at(row, col, dr, f, e), tile_at(row, col, -dr, -f, -e)
        copy = far_copy(CLOSE + i, target, edge_send.at[i], edge_recv.at[i])
        return target, jnp.logical_not(touches(dr, target)), jnp.logical_not(touches(-dr, origin)), copy

    for i in range(len(EDGE)):
        target, sends, receives, copy = edge(i)

        @pl.when(sends)
        def _(i=i, target=target, copy=copy):
            fill(CLOSE + i, target)
            copy.start()

        @pl.when(jnp.logical_not(receives))
        def _(i=i):
            far_ref[CLOSE + i] = jnp.zeros(far_ref.shape[1:], far_ref.dtype)

    far_ref[UNUSED] = jnp.zeros(far_ref.shape[1:], far_ref.dtype)

    def pack(source, first, count, right, target):
        for r in range(count):
            if right:
                edge = source[first + r, TW - 16:].astype(jnp.float32)[16 - R:]
            else:
                edge = source[first + r, :16].astype(jnp.float32)[:R]
            pack_ref[pl.ds(r * R, R)] = edge
        if target.shape[0] > count * R:
            pack_ref[count * R:target.shape[0]] = jnp.zeros((target.shape[0] - count * R, pack_ref.shape[1]), jnp.float32)
        target[...] = pack_ref[:target.shape[0]].astype(jnp.bfloat16)

    loads[2].wait()
    loads[3].wait()
    for i, (ref, right) in enumerate(((k_ref, True), (v_ref, True), (k_ref, False), (v_ref, False))):
        pack(ref, 0, TH, right, side_ref.at[i])
    start_halo(WEST)
    start_halo(EAST)
    for i, piece in enumerate((NW, NE, SW, SE)):
        @pl.when(crossing[piece])
        def _(i=i, piece=piece):
            for n, ref in enumerate((k_ref, v_ref)):
                pack(ref, TH - R if piece in (NW, NE) else 0, R, piece in (NW, SW), corner_ref.at[2 * i + n])
        start_halo(piece, True)

    def clear(missing, refs):
        @pl.when(missing)
        def _():
            for ref in refs:
                ref[...] = jnp.zeros(ref.shape, ref.dtype)

    top, middle, bottom = pl.ds(0, CORNER), pl.ds(CORNER, SIDE), pl.ds(CORNER + SIDE, CORNER)
    clear(jnp.logical_not(has_n), [kn_ref, vn_ref])
    clear(jnp.logical_not(has_s), [ks_ref, vs_ref])
    clear(jnp.logical_not(has_w), [kw_ref.at[middle], vw_ref.at[middle]])
    clear(jnp.logical_not(has_e), [ke_ref.at[middle], ve_ref.at[middle]])
    clear(jnp.logical_not(exists[NW]), [kw_ref.at[top], vw_ref.at[top]])
    clear(jnp.logical_not(exists[SW]), [kw_ref.at[bottom], vw_ref.at[bottom]])
    clear(jnp.logical_not(exists[NE]), [ke_ref.at[top], ve_ref.at[top]])
    clear(jnp.logical_not(exists[SE]), [ke_ref.at[bottom], ve_ref.at[bottom]])

    def key_marks(shape, place):
        u, v, real = place(shape)
        lane = lax.broadcasted_iota(jnp.int32, shape, len(shape) - 1)
        on = (lane == u + R + ROW_AT) | (lane == v + R + COL_AT) | ((lane == PAD_AT) & jnp.logical_not(real))
        return jnp.where(on, 1.0, 0.0).reshape(-1, HD).astype(jnp.bfloat16)

    def make_query_marks():
        shape = (HD, TH * TW)
        lane = lax.broadcasted_iota(jnp.int32, shape, 0)
        query = lax.broadcasted_iota(jnp.int32, (1, TH * TW), 1)
        query_row, query_col = query // TW, query % TW
        u, v = lane - ROW_AT - R, lane - COL_AT - R
        row_off = (jnp.abs(u - query_row) > R) | (u + row * TH < 0) | (u + row * TH >= ROWS * TH)
        col_off = (jnp.abs(v - query_col) > R) | (v + col * TW < 0) | (v + col * TW >= COLS * TW)
        low = ((lane < COL_AT) & row_off) | ((lane >= COL_AT) & (lane < PAD_AT) & col_off) | (lane == PAD_AT)
        return jnp.where(low, LOW, jnp.where(lane == DEAD_AT, 1.0, 0.0)).astype(jnp.bfloat16)

    def strip_place(first_col):
        def place(shape):
            key = lax.broadcasted_iota(jnp.int32, shape, 0)
            upper, lower = key < CORNER, key >= CORNER + SIDE
            start = jnp.where(upper, 0, jnp.where(lower, CORNER + SIDE, CORNER))
            first_row = jnp.where(upper, -R, jnp.where(lower, TH, 0))
            cell = key - start
            real = (cell < R * R) | jnp.logical_not(upper | lower)
            return first_row + cell // R, first_col + cell % R, real

        return place

    def band_place(first_row):
        def place(shape):
            u, v = (lax.broadcasted_iota(jnp.int32, shape, axis) for axis in (0, 1))
            return first_row + u, v, v >= 0

        return place

    own_marks[...] = key_marks((TH, TW, HD), band_place(0))

    def lanes(h):
        return pl.ds(pl.multiple_of(h * HD, HD), HD)

    def across(half):
        return pl.ds(0, 2 * HALF) if half is None else pl.ds(half * HALF, HALF)

    def scores(keys, query):
        return jnp.dot(keys, query, preferred_element_type=jnp.float32)

    def mix(values, weights):
        return lax.dot_general(values, weights, (((0,), (0,)), ((), ())), preferred_element_type=jnp.float32)

    def absorb(h0, parts_of, first=False, halves=(0, 1), last=False):
        chains = [(h0 + i, half) for i in (0, 1) for half in halves]

        def start(chain):
            h, half = chain
            query = qt_ref[h, :, across(half)]
            parts = parts_of(h, half)
            return [(scores(jnp.concatenate([keys, marks], axis=1), query), values) for keys, marks, values in parts]

        def finish(chain, parts):
            h, half = chain
            peak = jnp.max(parts[0][0], axis=0, keepdims=True)
            for raw, _ in parts[1:]:
                peak = jnp.maximum(peak, jnp.max(raw, axis=0, keepdims=True))
            if not first:
                before = m_ref[h, :, across(half)]
                peak = jnp.maximum(before, peak)
            total, mixed = None, None
            for raw, values in parts:
                weights = jnp.exp2((raw - peak) * SCALE)
                part = jnp.sum(weights, axis=0, keepdims=True)
                product = mix(values, weights.astype(jnp.bfloat16))
                total = part if total is None else total + part
                mixed = product if mixed is None else mixed + product
            if not first:
                fade = jnp.exp2((before - peak) * SCALE)
                total = l_ref[h, :, across(half)] * fade + total
                mixed = acc_ref[h, :, across(half)] * fade + mixed
            return peak, total, mixed

        results = []
        ready = start(chains[0])
        for n, chain in enumerate(chains):
            parts = ready
            if n + 1 < len(chains):
                ready = start(chains[n + 1])
            results.append(finish(chain, parts))
        if last:
            for (h, half), (_, total, mixed) in zip(chains, results):
                att_ref[across(half), lanes(h)] = (mixed / total).T.astype(jnp.bfloat16)
            return
        for (h, half), found in zip(chains, results):
            m_ref[h, :, across(half)], l_ref[h, :, across(half)], acc_ref[h, :, across(half)] = found

    loads[4].wait()
    marks_t = make_query_marks()

    @pl.loop(0, heads)
    def _(h):
        qt_ref[h, :HD] = q_ref[:, lanes(h)].astype(jnp.float32).T.astype(jnp.bfloat16)
        qt_ref[h, HD:] = marks_t

    @pl.loop(0, heads, step=2)
    def _(h0):
        @pl.loop(0, 4)
        def _(j):
            slot = AHEAD + 2 * h0 + j
            send_far(slot, close_offset(slot), 0)

        def parts_of(h, half):
            rows = pl.ds(half * 2, TH - 2)
            keys = k_ref[rows, :, lanes(h)].reshape(OWN_SPAN, HD)
            return [(keys, own_marks[pl.ds(half * 2 * TW, OWN_SPAN)], v_ref[rows, :, lanes(h)].reshape(OWN_SPAN, HD))]

        absorb(h0, parts_of, first=True)

    west_marks[...] = key_marks((STRIP, HD), strip_place(-R))
    east_marks[...] = key_marks((STRIP, HD), strip_place(TW))
    north_marks[...] = key_marks((R, TW, HD), band_place(-R))
    south_marks[...] = key_marks((R, TW, HD), band_place(TH))

    def far_sources():
        slot = lax.broadcasted_iota(jnp.int32, (1, SLOTS), 1)
        found = [
            jnp.where(slot < CLOSE, first, jnp.where(slot < MAIN, second, third))
            for first, second, third in zip(close_offset(slot), edge_offset(slot - CLOSE), main_offset(slot - MAIN))
        ]
        source = tile_at(row, col, *(-part for part in found))
        return jnp.where(slot == UNUSED, -2, source[0] * COLS + source[1]).astype(jnp.float32)

    tile = lax.broadcasted_iota(jnp.int32, far_lists.shape, 1)
    own_list = jnp.max(jnp.where(tile == row * COLS + col, far_lists[...].astype(jnp.float32), -1.0), axis=1, keepdims=True)
    listed = jnp.max(jnp.where(far_sources() == own_list, 0.0, LOW).astype(jnp.float32), axis=0, keepdims=True)
    live_ref[...] = jnp.broadcast_to(listed, live_ref.shape).T

    @pl.loop(0, SLOTS // 2)
    def _(pair):
        both = [jnp.broadcast_to(live_ref[pl.ds(2 * pair + i, 1), :], (BLK, HD)) for i in (0, 1)]
        lane = lax.broadcasted_iota(jnp.int32, (2 * BLK, HD), 1)
        marks = jnp.where(lane == DEAD_AT, jnp.concatenate(both, axis=0), 0.0)
        far_marks[pl.ds(pl.multiple_of(pair * 2 * BLK, 2 * BLK), 2 * BLK)] = marks.astype(jnp.bfloat16)

    def use_far(group):
        first, count = GROUPS[group]
        regular = CLOSE if group == 0 else count
        part = far_ref.at[pl.ds(first, regular)]
        pltpu.make_async_remote_copy(
            src_ref=part, dst_ref=part, send_sem=far_send, recv_sem=far_recv.at[group],
            device_id=(row, (col + 1) % COLS), device_id_type=MESH,
        ).wait_recv()
        if group == 0:
            for i in range(len(EDGE)):
                _, _, receives, copy = edge(i)

                @pl.when(receives)
                def _(copy=copy):
                    copy.wait_recv()

        @pl.loop(first // 2, (first + count) // 2)
        def _(pair):
            rows = pl.ds(pl.multiple_of(pair * 2 * BLK, 2 * BLK), 2 * BLK)
            one, two = far_ref[2 * pair].astype(jnp.float32), far_ref[2 * pair + 1].astype(jnp.float32)
            far_k[rows] = jnp.concatenate([one[:BLK], two[:BLK]], axis=0).astype(jnp.bfloat16)
            far_v[rows] = jnp.concatenate([one[BLK:], two[BLK:]], axis=0).astype(jnp.bfloat16)

        @pl.loop(0, heads, step=2)
        def _(h0):
            rows = pl.ds(first * BLK, count * BLK)
            absorb(h0, lambda h, half: [(far_k[rows, lanes(h)], far_marks[rows], far_v[rows, lanes(h)])],
                   halves=(None,), last=group == len(GROUPS) - 1)

    use_far(0)
    wait_halo(NORTH)
    wait_halo(SOUTH)
    for i, piece in enumerate((NW, NE, SW, SE)):
        @pl.when(jnp.logical_not(crossing[piece]))
        def _(i=i, piece=piece):
            for n, ref in enumerate((kn_ref, vn_ref) if piece in (NW, NE) else (ks_ref, vs_ref)):
                pack(ref, 0, R, piece in (NW, SW), corner_ref.at[2 * i + n])
        start_halo(piece)

    @pl.loop(0, N_MAIN)
    def _(p):
        send_main(p)

    wait_halo(WEST)
    wait_halo(EAST)

    @pl.loop(0, heads, step=2)
    def _(h0):
        def parts_of(h, half):
            band_k, band_v, marks = ((kn_ref, vn_ref, north_marks), (ks_ref, vs_ref, south_marks))[half]
            found = [(band_k[:, :, lanes(h)].reshape(BAND, HD), marks[...], band_v[:, :, lanes(h)].reshape(BAND, HD))]
            for strip_k, strip_v, marks in ((kw_ref, vw_ref, west_marks), (ke_ref, ve_ref, east_marks)):
                found.append((strip_k[middle, lanes(h)], marks[middle], strip_v[middle, lanes(h)]))
            return found

        absorb(h0, parts_of)

    use_far(1)
    use_far(2)
    for piece in (NW, NE, SW, SE):
        wait_halo(piece)

    @pl.loop(0, heads, step=2)
    def _(h0):
        def parts_of(h, half):
            end = (top, bottom)[half]
            return [
                (strip_k[end, lanes(h)], marks[end], strip_v[end, lanes(h)])
                for strip_k, strip_v, marks in ((kw_ref, vw_ref, west_marks), (ke_ref, ve_ref, east_marks))
            ]

        absorb(h0, parts_of)

    use_far(3)

    out_copy = pltpu.make_async_copy(att_ref, att_hbm, out_sem)
    out_copy.start()

    for piece in range(8):
        wait_halo_sent(piece)
        if piece in crossing:
            wait_halo_sent(piece, True)
    sent = stage_ref.at[pl.ds(0, CLOSE + N_MAIN)]
    pltpu.make_async_remote_copy(
        src_ref=sent, dst_ref=sent, send_sem=far_send, recv_sem=far_recv.at[0],
        device_id=(row, (col + 1) % COLS), device_id_type=MESH,
    ).wait_send()
    for i in range(len(EDGE)):
        _, sends, _, copy = edge(i)

        @pl.when(sends)
        def _(copy=copy):
            copy.wait_send()
    out_copy.wait()


def shards(
    queries, fresh_keys, fresh_values, stale_keys, stale_values, weight_out, gate, far_tiles, far_blocks, far_count
):
    inner = queries.shape[2]
    heads = inner // HD
    model = weight_out.shape[1]
    own = lax.axis_index("row") * COLS + lax.axis_index("col")
    block_of = jnp.sum(jnp.where(far_tiles == own, far_blocks, 0), axis=1)

    bf16, f32 = jnp.bfloat16, jnp.float32
    tokens = TH * TW
    any_spec = pl.BlockSpec(memory_space=pl.ANY)
    vmem_spec = pl.BlockSpec(memory_space=pltpu.VMEM)
    smem_spec = pl.BlockSpec(memory_space=pltpu.SMEM)
    band, strip = (R, TW, inner), (STRIP, inner)
    attended = pl.pallas_call(
        kernel,
        out_shape=jax.ShapeDtypeStruct((tokens, inner), bf16),
        in_specs=[any_spec] * 5 + [vmem_spec, smem_spec],
        out_specs=any_spec,
        scratch_shapes=[
            pltpu.VMEM((tokens, inner), bf16),
            pltpu.VMEM((TH, TW, inner), bf16),
            pltpu.VMEM((TH, TW, inner), bf16),
            pltpu.VMEM((tokens // 16, 16, inner), bf16),
            pltpu.VMEM((tokens // 16, 16, inner), bf16),
            pltpu.VMEM(band, bf16), pltpu.VMEM(band, bf16), pltpu.VMEM(strip, bf16), pltpu.VMEM(strip, bf16),
            pltpu.VMEM(band, bf16), pltpu.VMEM(band, bf16), pltpu.VMEM(strip, bf16), pltpu.VMEM(strip, bf16),
            pltpu.VMEM((SIDE, inner), f32),
            pltpu.VMEM((4, SIDE, inner), bf16),
            pltpu.VMEM((8, CORNER, inner), bf16),
            pltpu.VMEM((SLOTS, 2 * BLK, inner), bf16),
            pltpu.VMEM((SLOTS, 2 * BLK, inner), bf16),
            pltpu.VMEM((heads, HD, tokens), f32),
            pltpu.VMEM((heads, 1, tokens), f32),
            pltpu.VMEM((heads, 1, tokens), f32),
            pltpu.VMEM((heads, 2 * HD, tokens), bf16),
            pltpu.VMEM((SLOTS * BLK, inner), bf16),
            pltpu.VMEM((SLOTS * BLK, inner), bf16),
            pltpu.VMEM((tokens, HD), bf16),
            pltpu.VMEM((BAND, HD), bf16),
            pltpu.VMEM((BAND, HD), bf16),
            pltpu.VMEM((STRIP, HD), bf16),
            pltpu.VMEM((STRIP, HD), bf16),
            pltpu.VMEM((SLOTS * BLK, HD), bf16),
            pltpu.VMEM((SLOTS, 128), f32),
            pltpu.VMEM((tokens, inner), bf16),
            pltpu.SemaphoreType.DMA((5,)),
            pltpu.SemaphoreType.DMA((16,)),
            pltpu.SemaphoreType.DMA((16,)),
            pltpu.SemaphoreType.DMA,
            pltpu.SemaphoreType.DMA((len(GROUPS),)),
            pltpu.SemaphoreType.DMA((len(EDGE),)),
            pltpu.SemaphoreType.DMA((len(EDGE),)),
            pltpu.SemaphoreType.DMA,
        ],
        compiler_params=pltpu.CompilerParams(has_side_effects=True, vmem_limit_bytes=52 * 1024 * 1024),
        name="attention",
    )(
        queries.reshape(tokens, inner), fresh_keys, fresh_values,
        stale_keys.reshape(-1, 16, inner), stale_values.reshape(-1, 16, inner), far_tiles.T, block_of,
    )
    projected = jnp.dot(attended, weight_out, preferred_element_type=jnp.float32)
    return (projected * gate[None, :]).astype(bf16).reshape(TH, TW, model)


def solution(mesh):
    tile = P("row", "col", None)
    return jax.shard_map(
        shards, mesh=mesh, in_specs=(tile,) * 5 + (P(),) * 5, out_specs=tile, check_vma=False,
    )
```

```python
import jax
import jax.numpy as jnp
from jax import lax
from jax.experimental import pallas as pl
from jax.experimental.pallas import tpu as pltpu
from jax.sharding import PartitionSpec as P

HD = 128
R = 6
BLK = 8
ROWS = 8
COLS = 16
TH = 16
TW = 32
HALF = 256
LOW = -1e30
SCALE = HD ** (-0.5) * 1.4426950408889634
MESH = pl.DeviceIdType.MESH

CLOSE = 29
EDGE = [(i, f, e) for i in (-1, 0, 1) for f in (0, 1) for e in (-1, 1)] + [(-1, 0, 0), (1, 0, 0)]
UNUSED = CLOSE + len(EDGE)
MAIN = UNUSED + 1
MIX = 25
SLOTS = 128
N_MAIN = SLOTS - MAIN
MID = COLS // 2
GROUPS = ((0, 48), (48, 32), (80, 32), (112, 16))
EARLY, BRIDGE = 4, 14


def blend(late, before, after):
    return before + late * (after - before)


def close_offset(j):
    dr = blend(j // 24, 2 + 2 * (j % 3), 0)
    e = blend(j // 24, j // 3, j - 22)
    return dr, 0, e


def edge_offset(i):
    last = i // 12
    return blend(last, i // 4 - 1, 2 * (i - 12) - 1), blend(last, i // 2 % 2, 0), blend(last, 2 * (i % 2) - 1, 0)


def main_offset(p):
    i = MIX * p % N_MAIN
    straight = i // 58
    k = i - 40
    e1 = blend(i // 40, i // 5, k // 3 + (k // 3 + 5) // 6)
    dr1 = blend(i // 40, 2 + i % 5, 7 + k % 3)
    k = i - 58
    e2 = blend(i // 74, k // 2, 2 + (k - 16) // 2)
    dr2 = blend(i // 74, 3 + 2 * (k % 2), 7 + 2 * (k % 2))
    return blend(straight, dr1, dr2), 1 - straight, blend(straight, e1, e2)


def tile_at(row, col, dr, f, e):
    return (row + dr + 2 * ROWS) % ROWS, (col // MID + f + 2) % 2 * MID + (col % MID + e + 2 * MID) % MID


ROW_AT, COL_AT, PAD_AT, DEAD_AT = 0, TH + 2 * R, TH + TW + 4 * R, TH + TW + 4 * R + 1

NORTH, SOUTH, WEST, EAST, NW, NE, SW, SE = range(8)
BAND = R * TW
CORNER = 48
SIDE = TH * R
STRIP = SIDE + 2 * CORNER
OWN_SPAN = (TH - 2) * TW


def kernel(
    q_hbm, k_hbm, v_hbm, sk_hbm, sv_hbm, far_lists, block_of, att_hbm,
    q_ref, k_ref, v_ref, sk_ref, sv_ref,
    kn_ref, ks_ref, kw_ref, ke_ref, vn_ref, vs_ref, vw_ref, ve_ref,
    pack_ref, side_ref, corner_ref,
    far_ref, stage_ref, acc_ref, m_ref, l_ref, qt_ref, far_k, far_v, own_marks, north_marks, south_marks, west_marks, east_marks, far_marks,
    live_ref, att_ref,
    load_sem, halo_send, halo_recv, far_send, far_recv, edge_send, edge_recv, out_sem,
):
    heads = q_ref.shape[1] // HD
    row = lax.axis_index("row")
    col = lax.axis_index("col")
    has_n, has_s = row > 0, row < ROWS - 1
    has_w, has_e = col > 0, col < COLS - 1
    exists = {
        NORTH: has_n, SOUTH: has_s, WEST: has_w, EAST: has_e,
        NW: has_n & has_w, NE: has_n & has_e, SW: has_s & has_w, SE: has_s & has_e,
    }

    crossing = {NW: col == MID - 1, SW: col == MID - 1, NE: col == MID, SE: col == MID}

    def halo_copies(piece, straight=False):
        up, down = (row - 1 + ROWS) % ROWS, (row + 1) % ROWS
        left, right = (col - 1 + COLS) % COLS, (col + 1) % COLS
        lower, upper = pl.ds(TH - R, R), pl.ds(0, R)
        top, middle, bottom = pl.ds(0, CORNER), pl.ds(CORNER, SIDE), pl.ds(CORNER + SIDE, CORNER)
        plan = {
            NORTH: (has_s, (down, col), (k_hbm.at[lower], v_hbm.at[lower]), (kn_ref, vn_ref)),
            SOUTH: (has_n, (up, col), (k_hbm.at[upper], v_hbm.at[upper]), (ks_ref, vs_ref)),
            WEST: (has_e, (row, right), (side_ref.at[0], side_ref.at[1]), (kw_ref.at[middle], vw_ref.at[middle])),
            EAST: (has_w, (row, left), (side_ref.at[2], side_ref.at[3]), (ke_ref.at[middle], ve_ref.at[middle])),
            NW: (has_n & has_e, (row, right), (corner_ref.at[0], corner_ref.at[1]), (kw_ref.at[top], vw_ref.at[top])),
            NE: (has_n & has_w, (row, left), (corner_ref.at[2], corner_ref.at[3]), (ke_ref.at[top], ve_ref.at[top])),
            SW: (has_s & has_e, (row, right), (corner_ref.at[4], corner_ref.at[5]),
                 (kw_ref.at[bottom], vw_ref.at[bottom])),
            SE: (has_s & has_w, (row, left), (corner_ref.at[6], corner_ref.at[7]),
                 (ke_ref.at[bottom], ve_ref.at[bottom])),
        }
        sends, target, srcs, dsts = plan[piece]
        if piece in crossing:
            if straight:
                sends = crossing[piece] & (has_s if piece in (NW, NE) else has_n)
                target = (down if piece in (NW, NE) else up, target[1])
            else:
                sends = sends & jnp.logical_not(crossing[piece])
        copies = [
            pltpu.make_async_remote_copy(
                src_ref=src, dst_ref=dst,
                send_sem=halo_send.at[2 * piece + i], recv_sem=halo_recv.at[2 * piece + i],
                device_id=target, device_id_type=MESH,
            )
            for i, (src, dst) in enumerate(zip(srcs, dsts))
        ]
        return sends, copies

    def start_halo(piece, straight=False):
        sends, copies = halo_copies(piece, straight)

        @pl.when(sends)
        def _():
            for copy in copies:
                copy.start()

    def wait_halo(piece):
        _, copies = halo_copies(piece)

        @pl.when(exists[piece])
        def _():
            for copy in copies:
                copy.wait_recv()

    def wait_halo_sent(piece, straight=False):
        sends, copies = halo_copies(piece, straight)

        @pl.when(sends)
        def _():
            for copy in copies:
                copy.wait_send()

    start_halo(NORTH)
    start_halo(SOUTH)

    loads = [
        pltpu.make_async_copy(src, dst, load_sem.at[i])
        for i, (src, dst) in enumerate(
            ((sk_hbm, sk_ref), (sv_hbm, sv_ref), (k_hbm, k_ref), (v_hbm, v_ref), (q_hbm, q_ref))
        )
    ]
    for load in loads:
        load.start()

    def far_copy(slot, target, send_sem, recv_sem):
        return pltpu.make_async_remote_copy(
            src_ref=stage_ref.at[slot], dst_ref=far_ref.at[slot], send_sem=send_sem, recv_sem=recv_sem,
            device_id=target, device_id_type=MESH,
        )

    def fill(slot, target):
        block = block_of[target[0] * COLS + target[1]]
        pair, odd = lax.shift_right_logical(block, 1), block & 1
        both = []
        for ref in (sk_ref, sv_ref):
            rows = ref[pair].astype(jnp.float32)
            both.append(jnp.where(odd == 1, rows[BLK:], rows[:BLK]))
        stage_ref[slot] = jnp.concatenate(both, axis=0).astype(jnp.bfloat16)

    def send_far(slot, offset, sem):
        target = tile_at(row, col, *offset)
        fill(slot, target)
        far_copy(slot, target, far_send, far_recv.at[sem]).start()

    loads[0].wait()
    loads[1].wait()

    @pl.loop(0, CLOSE)
    def _(j):
        send_far(j, close_offset(j), 0)

    def send_main(p):
        send_far(MAIN + p, main_offset(p), (MAIN + p - 16) // 32)

    for p in range(EARLY):
        send_main(p)

    def touches(dr, other):
        return (row + dr >= 0) & (row + dr < ROWS) & (other[1] - col >= -1) & (other[1] - col <= 1)

    def edge(i):
        dr, f, e = EDGE[i]
        target, origin = tile_at(row, col, dr, f, e), tile_at(row, col, -dr, -f, -e)
        copy = far_copy(CLOSE + i, target, edge_send.at[i], edge_recv.at[i])
        return target, jnp.logical_not(touches(dr, target)), jnp.logical_not(touches(-dr, origin)), copy

    for i in range(len(EDGE)):
        target, sends, receives, copy = edge(i)

        @pl.when(sends)
        def _(i=i, target=target, copy=copy):
            fill(CLOSE + i, target)
            copy.start()

        @pl.when(jnp.logical_not(receives))
        def _(i=i):
            far_ref[CLOSE + i] = jnp.zeros(far_ref.shape[1:], far_ref.dtype)

    far_ref[UNUSED] = jnp.zeros(far_ref.shape[1:], far_ref.dtype)

    def pack(source, first, count, right, target):
        for r in range(count):
            if right:
                edge = source[first + r, TW - 16:].astype(jnp.float32)[16 - R:]
            else:
                edge = source[first + r, :16].astype(jnp.float32)[:R]
            pack_ref[pl.ds(r * R, R)] = edge
        if target.shape[0] > count * R:
            pack_ref[count * R:target.shape[0]] = jnp.zeros((target.shape[0] - count * R, pack_ref.shape[1]), jnp.float32)
        target[...] = pack_ref[:target.shape[0]].astype(jnp.bfloat16)

    loads[2].wait()
    loads[3].wait()
    for i, (ref, right) in enumerate(((k_ref, True), (v_ref, True), (k_ref, False), (v_ref, False))):
        pack(ref, 0, TH, right, side_ref.at[i])
    start_halo(WEST)
    start_halo(EAST)
    for i, piece in enumerate((NW, NE, SW, SE)):
        @pl.when(crossing[piece])
        def _(i=i, piece=piece):
            for n, ref in enumerate((k_ref, v_ref)):
                pack(ref, TH - R if piece in (NW, NE) else 0, R, piece in (NW, SW), corner_ref.at[2 * i + n])
        start_halo(piece, True)

    def clear(missing, refs):
        @pl.when(missing)
        def _():
            for ref in refs:
                ref[...] = jnp.zeros(ref.shape, ref.dtype)

    top, middle, bottom = pl.ds(0, CORNER), pl.ds(CORNER, SIDE), pl.ds(CORNER + SIDE, CORNER)
    clear(jnp.logical_not(has_n), [kn_ref, vn_ref])
    clear(jnp.logical_not(has_s), [ks_ref, vs_ref])
    clear(jnp.logical_not(has_w), [kw_ref.at[middle], vw_ref.at[middle]])
    clear(jnp.logical_not(has_e), [ke_ref.at[middle], ve_ref.at[middle]])
    clear(jnp.logical_not(exists[NW]), [kw_ref.at[top], vw_ref.at[top]])
    clear(jnp.logical_not(exists[SW]), [kw_ref.at[bottom], vw_ref.at[bottom]])
    clear(jnp.logical_not(exists[NE]), [ke_ref.at[top], ve_ref.at[top]])
    clear(jnp.logical_not(exists[SE]), [ke_ref.at[bottom], ve_ref.at[bottom]])

    def key_marks(shape, place):
        u, v, real = place(shape)
        lane = lax.broadcasted_iota(jnp.int32, shape, len(shape) - 1)
        on = (lane == u + R + ROW_AT) | (lane == v + R + COL_AT) | ((lane == PAD_AT) & jnp.logical_not(real))
        return jnp.where(on, 1.0, 0.0).reshape(-1, HD).astype(jnp.bfloat16)

    def make_query_marks():
        shape = (HD, TH * TW)
        lane = lax.broadcasted_iota(jnp.int32, shape, 0)
        query = lax.broadcasted_iota(jnp.int32, (1, TH * TW), 1)
        query_row, query_col = query // TW, query % TW
        u, v = lane - ROW_AT - R, lane - COL_AT - R
        row_off = (jnp.abs(u - query_row) > R) | (u + row * TH < 0) | (u + row * TH >= ROWS * TH)
        col_off = (jnp.abs(v - query_col) > R) | (v + col * TW < 0) | (v + col * TW >= COLS * TW)
        low = ((lane < COL_AT) & row_off) | ((lane >= COL_AT) & (lane < PAD_AT) & col_off) | (lane == PAD_AT)
        return jnp.where(low, LOW, jnp.where(lane == DEAD_AT, 1.0, 0.0)).astype(jnp.bfloat16)

    def strip_place(first_col):
        def place(shape):
            key = lax.broadcasted_iota(jnp.int32, shape, 0)
            upper, lower = key < CORNER, key >= CORNER + SIDE
            start = jnp.where(upper, 0, jnp.where(lower, CORNER + SIDE, CORNER))
            first_row = jnp.where(upper, -R, jnp.where(lower, TH, 0))
            cell = key - start
            real = (cell < R * R) | jnp.logical_not(upper | lower)
            return first_row + cell // R, first_col + cell % R, real

        return place

    def band_place(first_row):
        def place(shape):
            u, v = (lax.broadcasted_iota(jnp.int32, shape, axis) for axis in (0, 1))
            return first_row + u, v, v >= 0

        return place

    own_marks[...] = key_marks((TH, TW, HD), band_place(0))

    def lanes(h):
        return pl.ds(pl.multiple_of(h * HD, HD), HD)

    def across(half):
        return pl.ds(0, 2 * HALF) if half is None else pl.ds(half * HALF, HALF)

    def scores(keys, query):
        return jnp.dot(keys, query, preferred_element_type=jnp.float32)

    def mix(values, weights):
        return lax.dot_general(values, weights, (((0,), (0,)), ((), ())), preferred_element_type=jnp.float32)

    def absorb(h0, parts_of, first=False, halves=(0, 1), last=False):
        chains = [(h0 + i, half) for i in (0, 1) for half in halves]

        def start(chain):
            h, half = chain
            query = qt_ref[h, :, across(half)]
            parts = parts_of(h, half)
            return [(scores(jnp.concatenate([keys, marks], axis=1), query), values) for keys, marks, values in parts]

        def finish(chain, parts):
            h, half = chain
            peak = jnp.max(parts[0][0], axis=0, keepdims=True)
            for raw, _ in parts[1:]:
                peak = jnp.maximum(peak, jnp.max(raw, axis=0, keepdims=True))
            if not first:
                before = m_ref[h, :, across(half)]
                peak = jnp.maximum(before, peak)
            total, mixed = None, None
            for raw, values in parts:
                weights = jnp.exp2((raw - peak) * SCALE)
                part = jnp.sum(weights, axis=0, keepdims=True)
                product = mix(values, weights.astype(jnp.bfloat16))
                total = part if total is None else total + part
                mixed = product if mixed is None else mixed + product
            if not first:
                fade = jnp.exp2((before - peak) * SCALE)
                total = l_ref[h, :, across(half)] * fade + total
                mixed = acc_ref[h, :, across(half)] * fade + mixed
            return peak, total, mixed

        results = []
        ready = start(chains[0])
        for n, chain in enumerate(chains):
            parts = ready
            if n + 1 < len(chains):
                ready = start(chains[n + 1])
            results.append(finish(chain, parts))
        if last:
            for (h, half), (_, total, mixed) in zip(chains, results):
                att_ref[across(half), lanes(h)] = (mixed / total).T.astype(jnp.bfloat16)
            return
        for (h, half), found in zip(chains, results):
            m_ref[h, :, across(half)], l_ref[h, :, across(half)], acc_ref[h, :, across(half)] = found

    loads[4].wait()
    marks_t = make_query_marks()

    @pl.loop(0, heads)
    def _(h):
        qt_ref[h, :HD] = q_ref[:, lanes(h)].astype(jnp.float32).T.astype(jnp.bfloat16)
        qt_ref[h, HD:] = marks_t

    @pl.loop(0, heads, step=2)
    def _(h0):
        def parts_of(h, half):
            rows = pl.ds(half * 2, TH - 2)
            keys = k_ref[rows, :, lanes(h)].reshape(OWN_SPAN, HD)
            return [(keys, own_marks[pl.ds(half * 2 * TW, OWN_SPAN)], v_ref[rows, :, lanes(h)].reshape(OWN_SPAN, HD))]

        absorb(h0, parts_of, first=True)

    west_marks[...] = key_marks((STRIP, HD), strip_place(-R))
    east_marks[...] = key_marks((STRIP, HD), strip_place(TW))
    north_marks[...] = key_marks((R, TW, HD), band_place(-R))
    south_marks[...] = key_marks((R, TW, HD), band_place(TH))

    def far_sources():
        slot = lax.broadcasted_iota(jnp.int32, (1, SLOTS), 1)
        found = [
            jnp.where(slot < CLOSE, first, jnp.where(slot < MAIN, second, third))
            for first, second, third in zip(close_offset(slot), edge_offset(slot - CLOSE), main_offset(slot - MAIN))
        ]
        source = tile_at(row, col, *(-part for part in found))
        return jnp.where(slot == UNUSED, -2, source[0] * COLS + source[1]).astype(jnp.float32)

    tile = lax.broadcasted_iota(jnp.int32, far_lists.shape, 1)
    own_list = jnp.max(jnp.where(tile == row * COLS + col, far_lists[...].astype(jnp.float32), -1.0), axis=1, keepdims=True)
    listed = jnp.max(jnp.where(far_sources() == own_list, 0.0, LOW).astype(jnp.float32), axis=0, keepdims=True)
    live_ref[...] = jnp.broadcast_to(listed, live_ref.shape).T

    @pl.loop(0, SLOTS // 2)
    def _(pair):
        both = [jnp.broadcast_to(live_ref[pl.ds(2 * pair + i, 1), :], (BLK, HD)) for i in (0, 1)]
        lane = lax.broadcasted_iota(jnp.int32, (2 * BLK, HD), 1)
        marks = jnp.where(lane == DEAD_AT, jnp.concatenate(both, axis=0), 0.0)
        far_marks[pl.ds(pl.multiple_of(pair * 2 * BLK, 2 * BLK), 2 * BLK)] = marks.astype(jnp.bfloat16)

    def use_far(group):
        first, count = GROUPS[group]
        regular = CLOSE + GROUPS[1][0] - MAIN if group == 0 else count
        part = far_ref.at[pl.ds(first, regular)]
        pltpu.make_async_remote_copy(
            src_ref=part, dst_ref=part, send_sem=far_send, recv_sem=far_recv.at[group],
            device_id=(row, (col + 1) % COLS), device_id_type=MESH,
        ).wait_recv()
        if group == 0:
            for i in range(len(EDGE)):
                _, _, receives, copy = edge(i)

                @pl.when(receives)
                def _(copy=copy):
                    copy.wait_recv()

        @pl.loop(first // 2, (first + count) // 2)
        def _(pair):
            rows = pl.ds(pl.multiple_of(pair * 2 * BLK, 2 * BLK), 2 * BLK)
            one, two = far_ref[2 * pair].astype(jnp.float32), far_ref[2 * pair + 1].astype(jnp.float32)
            far_k[rows] = jnp.concatenate([one[:BLK], two[:BLK]], axis=0).astype(jnp.bfloat16)
            far_v[rows] = jnp.concatenate([one[BLK:], two[BLK:]], axis=0).astype(jnp.bfloat16)

        @pl.loop(0, heads, step=2)
        def _(h0):
            rows = pl.ds(first * BLK, count * BLK)
            absorb(h0, lambda h, half: [(far_k[rows, lanes(h)], far_marks[rows], far_v[rows, lanes(h)])],
                   halves=(None,), last=group == len(GROUPS) - 1)

    use_far(0)

    @pl.loop(EARLY, BRIDGE)
    def _(p):
        send_main(p)

    wait_halo(NORTH)
    wait_halo(SOUTH)
    for i, piece in enumerate((NW, NE, SW, SE)):
        @pl.when(jnp.logical_not(crossing[piece]))
        def _(i=i, piece=piece):
            for n, ref in enumerate((kn_ref, vn_ref) if piece in (NW, NE) else (ks_ref, vs_ref)):
                pack(ref, 0, R, piece in (NW, SW), corner_ref.at[2 * i + n])
        start_halo(piece)

    @pl.loop(BRIDGE, N_MAIN)
    def _(p):
        send_main(p)

    wait_halo(WEST)
    wait_halo(EAST)

    @pl.loop(0, heads, step=2)
    def _(h0):
        def parts_of(h, half):
            band_k, band_v, marks = ((kn_ref, vn_ref, north_marks), (ks_ref, vs_ref, south_marks))[half]
            found = [(band_k[:, :, lanes(h)].reshape(BAND, HD), marks[...], band_v[:, :, lanes(h)].reshape(BAND, HD))]
            for strip_k, strip_v, marks in ((kw_ref, vw_ref, west_marks), (ke_ref, ve_ref, east_marks)):
                found.append((strip_k[middle, lanes(h)], marks[middle], strip_v[middle, lanes(h)]))
            return found

        absorb(h0, parts_of)

    use_far(1)
    use_far(2)
    for piece in (NW, NE, SW, SE):
        wait_halo(piece)

    @pl.loop(0, heads, step=2)
    def _(h0):
        def parts_of(h, half):
            end = (top, bottom)[half]
            return [
                (strip_k[end, lanes(h)], marks[end], strip_v[end, lanes(h)])
                for strip_k, strip_v, marks in ((kw_ref, vw_ref, west_marks), (ke_ref, ve_ref, east_marks))
            ]

        absorb(h0, parts_of)

    use_far(3)

    out_copy = pltpu.make_async_copy(att_ref, att_hbm, out_sem)
    out_copy.start()

    for piece in range(8):
        wait_halo_sent(piece)
        if piece in crossing:
            wait_halo_sent(piece, True)
    sent = stage_ref.at[pl.ds(0, CLOSE + N_MAIN)]
    pltpu.make_async_remote_copy(
        src_ref=sent, dst_ref=sent, send_sem=far_send, recv_sem=far_recv.at[0],
        device_id=(row, (col + 1) % COLS), device_id_type=MESH,
    ).wait_send()
    for i in range(len(EDGE)):
        _, sends, _, copy = edge(i)

        @pl.when(sends)
        def _(copy=copy):
            copy.wait_send()
    out_copy.wait()


def shards(
    queries, fresh_keys, fresh_values, stale_keys, stale_values, weight_out, gate, far_tiles, far_blocks, far_count
):
    inner = queries.shape[2]
    heads = inner // HD
    model = weight_out.shape[1]
    own = lax.axis_index("row") * COLS + lax.axis_index("col")
    block_of = jnp.sum(jnp.where(far_tiles == own, far_blocks, 0), axis=1)

    bf16, f32 = jnp.bfloat16, jnp.float32
    tokens = TH * TW
    any_spec = pl.BlockSpec(memory_space=pl.ANY)
    vmem_spec = pl.BlockSpec(memory_space=pltpu.VMEM)
    smem_spec = pl.BlockSpec(memory_space=pltpu.SMEM)
    band, strip = (R, TW, inner), (STRIP, inner)
    attended = pl.pallas_call(
        kernel,
        out_shape=jax.ShapeDtypeStruct((tokens, inner), bf16),
        in_specs=[any_spec] * 5 + [vmem_spec, smem_spec],
        out_specs=any_spec,
        scratch_shapes=[
            pltpu.VMEM((tokens, inner), bf16),
            pltpu.VMEM((TH, TW, inner), bf16),
            pltpu.VMEM((TH, TW, inner), bf16),
            pltpu.VMEM((tokens // 16, 16, inner), bf16),
            pltpu.VMEM((tokens // 16, 16, inner), bf16),
            pltpu.VMEM(band, bf16), pltpu.VMEM(band, bf16), pltpu.VMEM(strip, bf16), pltpu.VMEM(strip, bf16),
            pltpu.VMEM(band, bf16), pltpu.VMEM(band, bf16), pltpu.VMEM(strip, bf16), pltpu.VMEM(strip, bf16),
            pltpu.VMEM((SIDE, inner), f32),
            pltpu.VMEM((4, SIDE, inner), bf16),
            pltpu.VMEM((8, CORNER, inner), bf16),
            pltpu.VMEM((SLOTS, 2 * BLK, inner), bf16),
            pltpu.VMEM((SLOTS, 2 * BLK, inner), bf16),
            pltpu.VMEM((heads, HD, tokens), f32),
            pltpu.VMEM((heads, 1, tokens), f32),
            pltpu.VMEM((heads, 1, tokens), f32),
            pltpu.VMEM((heads, 2 * HD, tokens), bf16),
            pltpu.VMEM((SLOTS * BLK, inner), bf16),
            pltpu.VMEM((SLOTS * BLK, inner), bf16),
            pltpu.VMEM((tokens, HD), bf16),
            pltpu.VMEM((BAND, HD), bf16),
            pltpu.VMEM((BAND, HD), bf16),
            pltpu.VMEM((STRIP, HD), bf16),
            pltpu.VMEM((STRIP, HD), bf16),
            pltpu.VMEM((SLOTS * BLK, HD), bf16),
            pltpu.VMEM((SLOTS, 128), f32),
            pltpu.VMEM((tokens, inner), bf16),
            pltpu.SemaphoreType.DMA((5,)),
            pltpu.SemaphoreType.DMA((16,)),
            pltpu.SemaphoreType.DMA((16,)),
            pltpu.SemaphoreType.DMA,
            pltpu.SemaphoreType.DMA((len(GROUPS),)),
            pltpu.SemaphoreType.DMA((len(EDGE),)),
            pltpu.SemaphoreType.DMA((len(EDGE),)),
            pltpu.SemaphoreType.DMA,
        ],
        compiler_params=pltpu.CompilerParams(has_side_effects=True, vmem_limit_bytes=52 * 1024 * 1024),
        name="attention",
    )(
        queries.reshape(tokens, inner), fresh_keys, fresh_values,
        stale_keys.reshape(-1, 16, inner), stale_values.reshape(-1, 16, inner), far_tiles.T, block_of,
    )
    projected = jnp.dot(attended, weight_out, preferred_element_type=jnp.float32)
    return (projected * gate[None, :]).astype(bf16).reshape(TH, TW, model)


def solution(mesh):
    tile = P("row", "col", None)
    return jax.shard_map(
        shards, mesh=mesh, in_specs=(tile,) * 5 + (P(),) * 5, out_specs=tile, check_vma=False,
    )
```
